128 devices in a mesh: dp: 4 (over y), pipe: 4 (over z), expert: 8 (over x, core).
Axes of the slice: x: 4, y: 4, z: 4, core: 2. Of those that a mesh axis runs over, the one named last changes fastest.
Arguments:
- tokens: bfloat16 [4, 4096, 5120], P('pipe', ('dp', 'expert')), may hold values from -6 to 6
- cotangent: bfloat16 [4, 4096, 5120], P('pipe', ('dp', 'expert')), may hold values from -6 to 6
- gain: float32 [4, 5120], P('pipe'), may hold values from 0.1 to 1.9
- w_gate: bfloat16 [4, 8, 5120, 768], P('pipe', 'expert', 'dp'), may hold values from -0.078125 to 0.078125
- w_up: bfloat16 [4, 8, 5120, 768], P('pipe', 'expert', 'dp'), may hold values from -0.078125 to 0.078125
- w_down: bfloat16 [4, 8, 768, 5120], P('pipe', 'expert', None, 'dp'), may hold values from -0.21875 to 0.21875
- route: int32 [4, 4, 512, 1], P('pipe', None, ('dp', 'expert')), may hold values from 0 to 7; in each aligned block of 16 rows (0 to 15, 16 to 31, ..., all dimensions but the last counted through in order) at most 3 rows name the same one
Outputs:
- out_tokens: bfloat16 [4, 4096, 5120], P('pipe', ('dp', 'expert'))
- grad_tokens: bfloat16 [4, 4096, 5120], P('pipe', ('dp', 'expert'))
- grad_gain: float32 [4, 5120], P('pipe')
- grad_gate: bfloat16 [4, 8, 5120, 768], P('pipe', 'expert', 'dp')
- grad_up: bfloat16 [4, 8, 5120, 768], P('pipe', 'expert', 'dp')
- grad_down: bfloat16 [4, 8, 768, 5120], P('pipe', 'expert', None, 'dp')
The draws below stay inside these ranges and needn't reach their ends.
Inputs may be any that keep to these rules, and one draw needn't show every extreme that they name: route[l, m, t, 0] is the expert of tile t at layer l for micro-batch m. Among the 16 tiles of one device for one layer and one micro-batch (aligned blocks), no expert is named more than 3 times; every expert is named somewhere.
All inputs are finite; a program needn't handle non-finite values.
Results may differ from the reference program's by a relative error of at most 0.034.
Values may be sent and summed in bfloat16 or wider, within the bound.
A program may use at most 128 MiB of HBM per device.

```python
import math
import jax
import jax.numpy as jnp
import numpy as np
from jax import lax

D = 5120
FF = 768
TILE = 8
TILES_MB = 16
PASSES = 2
EXPERTS = 8
CAP = 3
ROWS = 4096
TILES = 512
N_DP = 4
N_PIPE = 4


def levels(stream_key, extent, split, least, top_value):
    def one(axis_at, parts):
        heights = jax.random.uniform(jax.random.fold_in(jax.random.fold_in(stream_key, 6), axis_at), (parts,), jnp.float32, least / len(split), top_value / len(split))
        return jnp.repeat(jnp.exp(heights), extent[axis_at] // parts).reshape((-1,) + (1,) * (len(extent) - axis_at - 1))

    level = one(*split[0])
    for cut in split[1:]:
        level = level * one(*cut)
    return level


def routed_block(own_key, own, number, rows, amount, top, most, skew):
    sequence = jax.random.permutation(own_key, amount)
    heavy_load, usual = portions_of(amount, rows * top, most, skew, True), portions_of(amount, rows * top, most, skew, False)
    places = jnp.arange(amount)

    def named(lengths, rotation):
        used = int((lengths > 0).sum())
        fixed = max(1, used // 4)
        shifted = fixed + (places - fixed + rotation * (used - fixed)) % max(1, amount - fixed)
        return jnp.zeros((amount,), jnp.int32).at[sequence[jnp.where(places < fixed, places, shifted)]].set(jnp.asarray(lengths, jnp.int32))

    lengths = jnp.where(number % 4 == 0, named(heavy_load, number // 4), named(usual, number - number // 4 - 1))
    mixed = jax.random.permutation(jax.random.fold_in(own, 3), amount)
    donor, taker = mixed[0:amount // 2 * 2:2], mixed[1:amount // 2 * 2:2]
    slack = jnp.minimum(lengths[donor] - 1, most - lengths[taker]) // 2
    slack = jnp.where((donor == sequence[0]) | (taker == sequence[0]) | (lengths[taker] == 0), 0, jnp.maximum(slack, 0))
    shifted = jax.random.randint(jax.random.fold_in(own, 4), (amount // 2,), 0, 1 << 20) % (slack + 1)
    lengths = lengths.at[donor].add(-shifted).at[taker].add(shifted)
    labels = jnp.searchsorted(jnp.cumsum(lengths), jnp.arange(rows * top), side="right").astype(jnp.int32)
    grid = labels.reshape(top, rows).T
    grid = grid[jax.random.permutation(jax.random.fold_in(own, 1), rows)]
    rotation = jax.random.randint(jax.random.fold_in(own, 2), (rows, 1), 0, top)
    return jnp.take_along_axis(grid, (jnp.arange(top)[None, :] + rotation) % top, axis=1)


def portions_of(number_of, total, limit, slope, full):
    portions = [(1 << 20) // math.isqrt(rank ** slope) + 1 for rank in range(1, number_of + 1)]
    largest = limit if full else min(limit, max(-(-total // number_of), total * portions[0] // sum(portions)))
    least = 1 if total - largest >= number_of - 1 else 0
    holding, surplus = [largest] + [least] * (number_of - 1), total - largest - least * (number_of - 1)
    while surplus > 0:
        candidates = [i for i in range(1, number_of) if holding[i] < largest] or [i for i in range(1, number_of) if holding[i] < limit]
        pool, budget = sum([portions[i] for i in candidates]), surplus
        for i in candidates:
            extra = min(limit - holding[i], max(1, budget * portions[i] // pool), surplus)
            holding[i] = holding[i] + extra
            surplus = surplus - extra
    return np.array(holding)


def gaussian(key, extent, scale, limit, pieces=(), kind=jnp.bfloat16):
    array = jax.random.normal(key, extent, jnp.float32) * scale
    if len(pieces) > 0:
        array = levels(key, extent, pieces, -0.22, 0.18) * array
    return jnp.clip(array, min=-limit, max=limit).astype(kind)


def setup_inputs(seed: int = 0) -> dict:
    streams_of = jax.random.split(jax.random.key(seed), 8)
    tokens = gaussian(streams_of[0], (N_PIPE, ROWS, D), 1.0, 6.0, ((0, 4), (1, 32)))
    cotangent = gaussian(streams_of[1], (N_PIPE, ROWS, D), 1.0, 6.0, ((0, 4), (1, 32)))
    gain = jnp.clip(1.0 + 0.18 * jax.random.normal(streams_of[2], (N_PIPE, D), jnp.float32), 0.1, 1.9)
    w_gate = gaussian(streams_of[3], (N_PIPE, EXPERTS, D, FF), D ** -0.5, 0.078125, ((0, 4), (1, 8), (2, 4)))
    w_up = gaussian(streams_of[4], (N_PIPE, EXPERTS, D, FF), D ** -0.5, 0.078125, ((0, 4), (1, 8), (2, 4)))
    w_down = gaussian(streams_of[5], (N_PIPE, EXPERTS, FF, D), FF ** -0.5, 0.21875, ((0, 4), (1, 8), (3, 4)))
    route_keys = jax.random.split(jax.random.fold_in(streams_of[6], 1), N_PIPE * N_PIPE * TILES // TILES_MB)
    route_turns = jax.random.permutation(jax.random.fold_in(streams_of[6], 3), N_PIPE * N_PIPE * TILES // TILES_MB)
    route = jax.vmap(lambda own, number: routed_block(jax.random.fold_in(streams_of[6], 2), own, number, TILES_MB, EXPERTS, 1, CAP, 2))(route_keys, route_turns).reshape((N_PIPE, N_PIPE, TILES, 1))
    return dict(tokens=tokens, cotangent=cotangent, gain=gain, w_gate=w_gate, w_up=w_up, w_down=w_down, route=route)


epsilon = 1e-06

def contract_last(former, latter):
    return lax.dot_general(former, latter, (((1,), (1,)), ((), ())), preferred_element_type=jnp.float32)

def contract_first(former, latter):
    return lax.dot_general(former, latter, (((0,), (0,)), ((), ())), preferred_element_type=jnp.float32)

def normalize(hidden, gain_row):
    widened = hidden.astype(jnp.float32)
    inverse = lax.rsqrt(lax.optimization_barrier(jnp.mean(widened * widened, axis=-1, keepdims=True)) + epsilon)
    scaled = widened * inverse
    return ((scaled * gain_row).astype(jnp.bfloat16), scaled, inverse)

def hidden_pair(rows_now, gate_weight, up_weight):
    quarter = rows_now.shape[1] // N_DP
    gate_pre = jnp.zeros((rows_now.shape[0], gate_weight.shape[1]), jnp.float32)
    up_pre = jnp.zeros((rows_now.shape[0], up_weight.shape[1]), jnp.float32)
    for part_index in range(N_DP):
        lower = part_index * quarter
        upper = lower + quarter
        gate_part = jnp.dot(rows_now[:, lower:upper], gate_weight[lower:upper], preferred_element_type=jnp.float32).astype(jnp.bfloat16)
        up_part = jnp.dot(rows_now[:, lower:upper], up_weight[lower:upper], preferred_element_type=jnp.float32).astype(jnp.bfloat16)
        gate_part, up_part = lax.optimization_barrier((gate_part, up_part))
        gate_pre = gate_pre + gate_part.astype(jnp.float32)
        up_pre = up_pre + up_part.astype(jnp.float32)
    return (gate_pre, up_pre)

def expert_forward(rows_now, gate_weight, up_weight, down_weight):
    gate_pre, up_pre = hidden_pair(rows_now, gate_weight, up_weight)
    activated = (jax.nn.silu(gate_pre) * up_pre).astype(jnp.bfloat16)
    return jnp.dot(activated, down_weight, preferred_element_type=jnp.float32).astype(jnp.bfloat16)

def expert_backward(rows_now, grad_now, gate_weight, up_weight, down_weight):
    gate_pre, up_pre = hidden_pair(rows_now, gate_weight, up_weight)
    sigmoid_gate = jax.nn.sigmoid(gate_pre)
    silu_gate = gate_pre * sigmoid_gate
    activated = (silu_gate * up_pre).astype(jnp.bfloat16)
    quarter = grad_now.shape[1] // N_DP
    grad_act = jnp.zeros(gate_pre.shape, jnp.float32)
    for part_index in range(N_DP):
        lower = part_index * quarter
        upper = lower + quarter
        partial_value = contract_last(grad_now[:, lower:upper], down_weight[:, lower:upper]).astype(jnp.bfloat16)
        grad_act = grad_act + lax.optimization_barrier(partial_value).astype(jnp.float32)
    grad_gate_pre = (grad_act * up_pre * sigmoid_gate * (1.0 + gate_pre * (1.0 - sigmoid_gate))).astype(jnp.bfloat16)
    grad_up_pre = (grad_act * silu_gate).astype(jnp.bfloat16)
    back_rows = (contract_last(grad_gate_pre, gate_weight) + contract_last(grad_up_pre, up_weight)).astype(jnp.bfloat16)
    grad_gate = contract_first(rows_now, grad_gate_pre)
    grad_up = contract_first(rows_now, grad_up_pre)
    grad_down = contract_first(activated, grad_now)
    return (back_rows, grad_gate, grad_up, grad_down)

def segments(tile_experts):
    tile_count = tile_experts.shape[0]
    per_block = math.gcd(tile_count, 8)
    block_count = tile_count // per_block
    blocked = tile_experts.reshape(block_count, per_block)
    lowest = blocked[:, 0].astype(jnp.int32)
    spread = (blocked[:, -1] - lowest + 1).astype(jnp.int32)
    begins = (jnp.cumsum(spread) - spread).astype(jnp.int32)
    seg_count = block_count + EXPERTS - 1
    positions = jnp.arange(seg_count, dtype=jnp.int32)
    owner_block = lax.optimization_barrier(jnp.sum((begins[None, :] <= positions[:, None]).astype(jnp.int32), axis=1)).astype(jnp.int32) - 1
    owner_block = jnp.clip(owner_block, 0, block_count - 1).astype(jnp.int32)
    expert_of = jnp.clip(lowest[owner_block] + positions - begins[owner_block], 0, EXPERTS - 1).astype(jnp.int32)
    usable = positions < jnp.sum(spread).astype(jnp.int32)
    return (per_block, block_count, owner_block, expert_of, usable)

def grouped_forward(tiles_sorted, tile_experts, gate_weight, up_weight, down_weight):
    per_block, block_count, owner_block, expert_of, usable = segments(tile_experts)
    model_width = tiles_sorted.shape[-1]
    blocks = tiles_sorted.reshape(block_count, per_block * TILE, model_width)
    row_owner = jnp.repeat(tile_experts.reshape(block_count, per_block), TILE, axis=1)

    def visit(result_buf, segment):
        block_index, expert_index, allowed = segment
        rows_now = blocks[block_index]
        chosen = (row_owner[block_index] == expert_index) & allowed
        produced = expert_forward(rows_now, gate_weight[expert_index], up_weight[expert_index], down_weight[expert_index]).astype(jnp.float32)
        result_buf = result_buf.at[block_index].add(jnp.where(chosen[:, None], produced, jnp.zeros_like(produced)))
        return (result_buf, None)
    start_buf = jnp.zeros((block_count, per_block * TILE, model_width), jnp.float32)
    result_buf, unused = lax.scan(visit, start_buf, (owner_block, expert_of, usable))
    return result_buf.reshape(-1, TILE, model_width).astype(jnp.bfloat16)

def grouped_backward(tiles_sorted, grads_sorted, tile_experts, gate_weight, up_weight, down_weight, sums):
    per_block, block_count, owner_block, expert_of, usable = segments(tile_experts)
    model_width = tiles_sorted.shape[-1]
    blocks = tiles_sorted.reshape(block_count, per_block * TILE, model_width)
    grad_blocks = grads_sorted.reshape(block_count, per_block * TILE, model_width)
    row_owner = jnp.repeat(tile_experts.reshape(block_count, per_block), TILE, axis=1)

    def visit(carry, segment):
        result_buf, acc_gate, acc_up, acc_down = carry
        block_index, expert_index, allowed = segment
        rows_now = blocks[block_index]
        chosen = (row_owner[block_index] == expert_index) & allowed
        grad_all = grad_blocks[block_index]
        grad_now = jnp.where(chosen[:, None], grad_all, jnp.zeros_like(grad_all))
        back_rows, part_gate, part_up, part_down = expert_backward(rows_now, grad_now, gate_weight[expert_index], up_weight[expert_index], down_weight[expert_index])
        back_wide = back_rows.astype(jnp.float32)
        result_buf = result_buf.at[block_index].add(jnp.where(chosen[:, None], back_wide, jnp.zeros_like(back_wide)))
        acc_gate = acc_gate.at[expert_index].add(part_gate)
        acc_up = acc_up.at[expert_index].add(part_up)
        acc_down = acc_down.at[expert_index].add(part_down)
        return ((result_buf, acc_gate, acc_up, acc_down), None)
    start_buf = jnp.zeros((block_count, per_block * TILE, model_width), jnp.float32)
    carry, unused = lax.scan(visit, (start_buf,) + tuple(sums), (owner_block, expert_of, usable))
    back_sorted = carry[0].reshape(-1, TILE, model_width).astype(jnp.bfloat16)
    return (back_sorted, carry[1:])

def layer_forward(hidden, gain_row, gate_weight, up_weight, down_weight, route_row):
    normed, scaled, inverse = normalize(hidden, gain_row)
    sort_order = jnp.argsort(route_row, stable=True).astype(jnp.int32)
    restore = jnp.argsort(sort_order, stable=True).astype(jnp.int32)
    tile_blocks = normed.reshape(-1, TILE, normed.shape[-1])
    produced = grouped_forward(tile_blocks[sort_order], route_row[sort_order], gate_weight, up_weight, down_weight)
    ffn_rows = produced[restore].reshape(hidden.shape)
    return (hidden.astype(jnp.float32) + ffn_rows.astype(jnp.float32)).astype(jnp.bfloat16)

def layer_backward(hidden, grad_rows, gain_row, gate_weight, up_weight, down_weight, route_row, sums):
    normed, scaled, inverse = normalize(hidden, gain_row)
    sort_order = jnp.argsort(route_row, stable=True).astype(jnp.int32)
    restore = jnp.argsort(sort_order, stable=True).astype(jnp.int32)
    tile_blocks = normed.reshape(-1, TILE, normed.shape[-1])
    grad_tiles = grad_rows.reshape(-1, TILE, grad_rows.shape[-1])
    back_sorted, sums = grouped_backward(tile_blocks[sort_order], grad_tiles[sort_order], route_row[sort_order], gate_weight, up_weight, down_weight, sums)
    grad_normed = back_sorted[restore].reshape(hidden.shape).astype(jnp.float32)
    gain_part = lax.optimization_barrier(jnp.sum(grad_normed * scaled, axis=0))
    grad_scaled = grad_normed * gain_row
    grad_wide = inverse * (grad_scaled - scaled * lax.optimization_barrier(jnp.mean(grad_scaled * scaled, axis=-1, keepdims=True)))
    grad_in = (grad_rows.astype(jnp.float32) + grad_wide).astype(jnp.bfloat16)
    return (grad_in, gain_part, sums)

def reference(tokens, cotangent, gain, w_gate, w_up, w_down, route):
    pipe_count = tokens.shape[0]
    stored = {}
    finals = [None] * pipe_count
    for micro_index in range(pipe_count):
        hidden = tokens[micro_index]
        for pass_index in range(PASSES):
            layer_index = (micro_index + pass_index) % pipe_count
            stored[micro_index, pass_index] = hidden
            hidden = layer_forward(hidden, gain[layer_index], w_gate[layer_index], w_up[layer_index], w_down[layer_index], route[layer_index, micro_index, :, 0])
        finals[(micro_index + PASSES - 1) % pipe_count] = hidden
    acc_gate = [jnp.zeros(w_gate.shape[1:], jnp.float32) for layer_index in range(pipe_count)]
    acc_up = [jnp.zeros(w_up.shape[1:], jnp.float32) for layer_index in range(pipe_count)]
    acc_down = [jnp.zeros(w_down.shape[1:], jnp.float32) for layer_index in range(pipe_count)]
    acc_gain = [jnp.zeros(gain.shape[1:], jnp.float32) for layer_index in range(pipe_count)]
    entry_grads = [None] * pipe_count
    for micro_index in range(pipe_count):
        grad_rows = cotangent[(micro_index + PASSES - 1) % pipe_count]
        for pass_index in reversed(range(PASSES)):
            layer_index = (micro_index + pass_index) % pipe_count
            grad_rows, gain_part, sums = layer_backward(stored[micro_index, pass_index], grad_rows, gain[layer_index], w_gate[layer_index], w_up[layer_index], w_down[layer_index], route[layer_index, micro_index, :, 0], (acc_gate[layer_index], acc_up[layer_index], acc_down[layer_index]))
            acc_gate[layer_index], acc_up[layer_index], acc_down[layer_index] = sums
            acc_gain[layer_index] = acc_gain[layer_index] + gain_part
        entry_grads[micro_index] = grad_rows
    return (jnp.stack(finals), jnp.stack(entry_grads), jnp.stack(acc_gain), jnp.stack([item.astype(jnp.bfloat16) for item in acc_gate]), jnp.stack([item.astype(jnp.bfloat16) for item in acc_up]), jnp.stack([item.astype(jnp.bfloat16) for item in acc_down]))
```

```python
import functools
import math

import jax
import jax.numpy as jnp
from jax import lax
from jax.experimental import pallas as pl
from jax.experimental.pallas import tpu as pltpu
from jax.sharding import PartitionSpec as P

TILE = 8
CAP = 3
PASSES = 2
WIDTH = 256
epsilon = 1e-06
F32 = jnp.float32
BF16 = jnp.bfloat16


def kernel(
    sizes,
    dest, tok, cot, gain, wg, wu, wd,
    out_tok, grad_tok, gain_out, gg, gu, gd,
    tokc, cotc, hid1, grad0, norm, wgu, wdc, dest_all, place, back,
    yin, xout, xin, acc, gate_up, act, act_t, grad_act,
    rs_f, rs_b, one_f, one_b, two_f, two_b,
    ret_out, ret_in, yret_out, yret_in, inverse, mean_acc, gain_acc, gain_dp, gain_ex, gain_all,
    load_sem, store_sem, dest_s, dest_r, y_s, y_r, x_s, x_r, rx_s, rx_r, ry_s, ry_r,
    z_s, z_r, ar_s, one_r, two_r, ag_r, gain_s, gain_r,
):
    nd, npipe, ne, rows, width, hidden = sizes
    quarter = width // nd
    kc = min(WIDTH, quarter)
    nk = quarter // kc
    block = nd * CAP * TILE
    total = ne * block
    half_ne = ne // 2
    group = total // 2
    part = group // nd
    half = part // 2
    q, p, e = lax.axis_index("dp"), lax.axis_index("pipe"), lax.axis_index("expert")
    chip, core = e // 2, lax.rem(e, 2)
    place_e = core * half_ne + chip
    q_up, q_down, q_far = lax.rem(q + 1, nd), lax.rem(q + nd - 1, nd), lax.rem(q + 2, nd)
    p_up, p_down = lax.rem(p + 1, npipe), lax.rem(p + npipe - 1, npipe)

    def send(src, dst, ssem, rsem, **where):
        pltpu.make_async_remote_copy(
            src_ref=src, dst_ref=dst, send_sem=ssem, recv_sem=rsem,
            device_id=where, device_id_type=pl.DeviceIdType.MESH,
        ).start()

    def drain(ref, sem):
        pltpu.make_async_copy(ref, ref, sem).wait()

    def loop(count, step):
        lax.fori_loop(0, count, lambda i, c: (step(i), c)[1], 0)

    def at(i, size):
        return pl.ds(pl.multiple_of(i * size, size), size)

    for k in range(nk):
        for j in range(nd):
            cols = pl.ds(j * quarter + k * kc, kc)
            pltpu.make_async_copy(tok.at[:, cols], tokc.at[k, j], load_sem.at[0]).start()
    pltpu.make_async_copy(wg, wgu.at[:, 0:hidden], load_sem.at[1]).start()
    pltpu.make_async_copy(wu, wgu.at[:, hidden : 2 * hidden], load_sem.at[1]).start()
    for k in range(nk):
        pltpu.make_async_copy(wd.at[:, pl.ds(k * kc, kc)], wdc.at[k], load_sem.at[2]).start()
    for k in range(nk):
        for j in range(nd):
            cols = pl.ds(j * quarter + k * kc, kc)
            pltpu.make_async_copy(cot.at[:, cols], cotc.at[k, j], load_sem.at[3]).start()

    barrier = pltpu.get_barrier_semaphore()

    def greet(**where):
        pl.semaphore_signal(barrier, inc=1, device_id=where, device_id_type=pl.DeviceIdType.MESH)

    for d in range(1, nd):
        greet(dp=lax.rem(q + d, nd))
    for d in range(1, ne):
        greet(expert=lax.rem(e + d, ne))
    greet(pipe=p_up)
    greet(pipe=p_down)

    drain(tokc, load_sem.at[0])

    def squares(ref, k, before):
        for j in range(nd):
            wide = ref[k, j].astype(F32)
            before = before + jnp.sum(wide * wide, axis=-1, keepdims=True)
        return before

    def normalize(t, ref, total_squares):
        inverse[t] = lax.rsqrt(total_squares / width + epsilon)

        def step(k):
            for j in range(nd):
                norm[k, j] = (ref[k, j].astype(F32) * inverse[t] * gain[k, j]).astype(BF16)

        loop(nk, step)

    none = jnp.zeros((rows, 1), F32)
    normalize(0, tokc, lax.fori_loop(0, nk, lambda k, c: squares(tokc, k, c), none))
    pl.semaphore_wait(barrier, nd - 1 + ne - 1 + 2)

    for d in range(1, nd):
        send(dest, dest_all.at[q], dest_s, dest_r, dp=lax.rem(q + d, nd))
    dest_all[q] = dest[...]

    def build_places():
        drain(dest_all.at[0 : nd - 1], dest_r)
        slot_ids = lax.broadcasted_iota(jnp.int32, (total, rows), 0).astype(F32)
        for t in range(PASSES):
            for s in range(nd):
                hot = jnp.where(slot_ids == dest_all[s, t, 0:1, :], 1.0, 0.0).astype(F32)
                place[t, :, s * rows : (s + 1) * rows] = hot.astype(BF16)
                back[t, s * rows : (s + 1) * rows, :] = hot.T.astype(BF16)

    tall = total // 3

    def y_send(ph, st, src, k):
        for d in range(1, nd):
            j = lax.rem(q + d, nd)
            send(src.at[k, j], yin.at[st, k, at(q, rows)], y_s.at[ph, k], y_r.at[ph, k], dp=j)
        yin[st, k, at(q, rows), :] = src[k, q]

    def x_send(ph, st, t, k):
        drain(yin.at[st, k, 0 : (nd - 1) * rows], y_r.at[ph, k])

        def some(m):
            xout[k, at(m, tall), :] = jnp.dot(
                place[t, at(m, tall), :], yin[st, k], preferred_element_type=F32
            ).astype(BF16)

        loop(3, some)
        for d in range(1, ne):
            o = lax.rem(e + d, ne)
            send(xout.at[k, at(o, block)], xin.at[ph, k, at(place_e, block)], x_s.at[ph, k], x_r.at[ph, k], expert=o)
        xin[ph, k, at(place_e, block), :] = xout[k, at(e, block), :]

    def forward_chunk(ph, k):
        drain(xin.at[ph, k, 0 : (ne - 1) * block], x_r.at[ph, k])

        def some(m):
            acc[at(m, tall), :] += jnp.dot(
                xin[ph, k, at(m, tall), :], wgu[at(k, kc), :], preferred_element_type=F32
            )

        loop(3, some)

    def backward_chunk(ph, k):
        drain(xin.at[ph, k, 0 : (ne - 1) * block], x_r.at[ph, k])

        def some(m):
            acc[at(m, tall), 0:hidden] += lax.dot_general(
                xin[ph, k, at(m, tall), :], wdc[k], (((1,), (1,)), ((), ())), preferred_element_type=F32
            )

        loop(3, some)

    def dispatch(ph, st, t, src, chunk, arrive=None, early=None):
        if arrive is None:
            loop(nk, lambda k: y_send(ph, st, src, k))
        if early is not None:
            early()
        acc[...] = jnp.zeros_like(acc)
        ahead = 0 if arrive is None else 1

        def step(i):
            if arrive is not None:

                @pl.when(i < nk)
                def _():
                    arrive(i)
                    y_send(ph, st, src, i)

            @pl.when((i >= ahead) & (i < nk + ahead))
            def _():
                x_send(ph, st, t, i - ahead)

            @pl.when(i >= ahead + 1)
            def _():
                chunk(ph, i - ahead - 1)

        loop(nk + 1 + ahead, step)

        def settle(k):
            drain(yin.at[st, k, 0 : (nd - 1) * rows], y_s.at[ph, k])
            drain(xout.at[k, 0 : (ne - 1) * block], x_s.at[ph, k])

        loop(nk, settle)

    def all_sum(ph, src, dst, one, two, columns):
        def span(g, b, h):
            return pl.ds(pl.multiple_of(g * group + b * part + h * half, half), half)

        def open_(g):
            send(src.at[span(g, q_far, 0)], one.at[g, 0], ar_s.at[ph, g, 0], one_r.at[ph, g, 0], dp=q_down)
            send(src.at[span(g, q_far, 1)], one.at[g, 1], ar_s.at[ph, g, 1], one_r.at[ph, g, 1], dp=q_up)
            send(src.at[span(g, q_down, 1)], two.at[g, 0, 1], ar_s.at[ph, g, 2], two_r.at[ph, g, 0, 1], dp=q_down)
            send(src.at[span(g, q_up, 0)], two.at[g, 1, 0], ar_s.at[ph, g, 3], two_r.at[ph, g, 1, 0], dp=q_up)

        def middle(g):
            for side, b in ((0, q_down), (1, q_up)):
                drain(one.at[g, side], one_r.at[ph, g, side])
                there = span(g, b, side)
                src[there, :] = (src[there, :].astype(F32) + one[g, side].astype(F32)).astype(BF16)
                send(src.at[there], two.at[g, side, side], ar_s.at[ph, g, 4 + side], two_r.at[ph, g, side, side], dp=b)

        def own(g):
            for h in range(2):
                for side in range(2):
                    drain(two.at[g, side, h], two_r.at[ph, g, side, h])
                mine = span(g, q, h)
                dst[mine, :] = (
                    src[mine, :].astype(F32) + two[g, 0, h].astype(F32) + two[g, 1, h].astype(F32)
                ).astype(BF16)
            for i in range(2):
                up, down = span(g, q, i), span(g, q, 1 - i)
                send(dst.at[up], dst.at[up], ar_s.at[ph, g, 6 + i], ag_r.at[ph, g, 0, i], dp=q_up)
                send(dst.at[down], dst.at[down], ar_s.at[ph, g, 8 + i], ag_r.at[ph, g, 1, 1 - i], dp=q_down)

        def pass_on(g):
            first, second = span(g, q_down, 0), span(g, q_up, 1)
            drain(dst.at[first], ag_r.at[ph, g, 0, 0])
            send(dst.at[first], dst.at[first], ar_s.at[ph, g, 10], ag_r.at[ph, g, 2, 0], dp=q_up)
            drain(dst.at[second], ag_r.at[ph, g, 1, 1])
            send(dst.at[second], dst.at[second], ar_s.at[ph, g, 11], ag_r.at[ph, g, 2, 1], dp=q_down)

        def close(g):
            drain(dst.at[span(g, q_down, 1)], ag_r.at[ph, g, 0, 1])
            drain(dst.at[span(g, q_up, 0)], ag_r.at[ph, g, 1, 0])
            drain(dst.at[span(g, q_far, 0)], ag_r.at[ph, g, 2, 0])
            drain(dst.at[span(g, q_far, 1)], ag_r.at[ph, g, 2, 1])

        def settle():
            for g in range(2):
                for i in range(12):
                    drain(src.at[0:half], ar_s.at[ph, g, i])

        return open_, middle, own, pass_on, close, settle

    def round_into(src, columns, g):
        def some(m):
            there = pl.ds(pl.multiple_of(g * group + m * half, half), half)
            src[there, :] = acc[there, 0:columns].astype(BF16)

        loop(group // half, some)

    def ret_send(ph, st, g, k):
        for i in range(half_ne):
            c = lax.rem(chip + i, half_ne)
            there = pl.ds(pl.multiple_of(g * group + c * block, block), block)
            landing = ret_in.at[st, k, at(e, block)]
            if i == 0:

                @pl.when(core != g)
                def _():
                    send(ret_out.at[k, there], landing, rx_s.at[ph, k], rx_r.at[ph, k], expert=2 * c + g)

                @pl.when(core == g)
                def _():
                    ret_in[st, k, at(e, block), :] = ret_out[k, there, :]
            else:
                send(ret_out.at[k, there], landing, rx_s.at[ph, k], rx_r.at[ph, k], expert=2 * c + g)

    short = nd * rows // 2

    def collect(ph, st, t, k):
        drain(ret_in.at[st, k, 0 : (ne - 1) * block], rx_r.at[ph, k])

        def some(m):
            yret_out[k, at(m, short), :] = jnp.dot(
                back[t, at(m, short), :], ret_in[st, k], preferred_element_type=F32
            ).astype(BF16)

        loop(2, some)
        for d in range(1, nd):
            j = lax.rem(q + d, nd)
            send(yret_out.at[k, at(j, rows)], yret_in.at[st, k, q], ry_s.at[ph, k], ry_r.at[ph, k], dp=j)
        yret_in[st, k, q] = yret_out[k, at(q, rows), :]

    def landed(ph, st, k):
        drain(yret_in.at[st, k, 0 : nd - 1], ry_r.at[ph, k])

    def settle_return(ph):
        def step(k):
            drain(ret_out.at[k, 0 : (ne - 1) * block], rx_s.at[ph, k])
            drain(yret_out.at[k, 0 : (nd - 1) * rows], ry_s.at[ph, k])

        loop(nk, step)

    def forward_expert(ph, t):
        open_, middle, own, pass_on, close, settle = all_sum(ph, rs_f, gate_up.at[t], one_f, two_f, 2 * hidden)
        for g in range(2):
            round_into(rs_f, 2 * hidden, g)
            open_(g)
        middle(0)
        middle(1)
        own(0)
        own(1)
        pass_on(0)
        pass_on(1)
        for g in range(2):
            close(g)

            def activate(m):
                there = pl.ds(pl.multiple_of(g * group + m * half, half), half)
                gate = gate_up[t, there, 0:hidden].astype(F32)
                up = gate_up[t, there, hidden : 2 * hidden].astype(F32)
                act[there, :] = (gate * jax.nn.sigmoid(gate) * up).astype(BF16)

            loop(group // half, activate)
            mine = slice(g * group, (g + 1) * group)

            def down(k):
                ret_out[k, mine, :] = jnp.dot(act[mine, :], wdc[k], preferred_element_type=F32).astype(BF16)
                ret_send(ph, 0, g, k)

            loop(nk, down)
        wide = math.gcd(total, 128)
        for m in range(total // wide):
            act_t[t, :, m * wide : (m + 1) * wide] = act[m * wide : (m + 1) * wide, :].T
        settle()

    def forward_return(ph, t, ref):
        def step(i):
            @pl.when(i < nk)
            def _():
                collect(ph, 0, t, i)

            @pl.when(i >= 1)
            def _():
                k = i - 1
                landed(ph, 0, k)
                for j in range(nd):
                    yret_in[0, k, j] = (ref[k, j].astype(F32) + yret_in[0, k, j].astype(F32)).astype(BF16)
                if t == 0:
                    send(yret_in.at[0, k], hid1.at[k], z_s.at[0, k], z_r.at[0, k], pipe=p_up)
                else:
                    for j in range(nd):
                        cols = pl.ds(pl.multiple_of(j * quarter + k * kc, kc), kc)
                        pltpu.make_async_copy(yret_in.at[0, k, j], out_tok.at[:, cols], store_sem.at[0]).start()

        loop(nk + 1, step)
        settle_return(ph)

    def backward_expert(ph, t):
        def pre(m):
            there = pl.ds(pl.multiple_of(m * half, half), half)
            gate = gate_up[t, there, 0:hidden].astype(F32)
            up = gate_up[t, there, hidden : 2 * hidden].astype(F32)
            grad = grad_act[there, :].astype(F32)
            s = jax.nn.sigmoid(gate)
            gate_up[t, there, 0:hidden] = (grad * up * s * (1.0 + gate * (1.0 - s))).astype(BF16)
            gate_up[t, there, hidden : 2 * hidden] = (grad * (gate * s)).astype(BF16)

        for g in range(2):
            lax.fori_loop(g * (group // half), (g + 1) * (group // half), lambda m, c: (pre(m), c)[1], 0)
            mine = slice(g * group, (g + 1) * group)

            def up_(k):
                ret_out[k, mine, :] = lax.dot_general(
                    gate_up[t, mine, :], wgu[at(k, kc), :], (((1,), (1,)), ((), ())), preferred_element_type=F32
                ).astype(BF16)
                ret_send(ph, 1, g, k)

            loop(nk, up_)

    def backward_return(ph, t, ref, grad_ref, beside):
        def terms(k, j):
            u = yret_in[1, k, j].astype(F32)
            return u, ref[k, j].astype(F32) * inverse[t]

        mean_acc[...] = jnp.zeros_like(mean_acc)

        def step(i):
            @pl.when(i < nk)
            def _():
                beside(i)
                collect(ph, 1, t, i)

            @pl.when(i >= 1)
            def _():
                k = i - 1
                landed(ph, 1, k)
                fresh = mean_acc[...]
                for j in range(nd):
                    u, scaled = terms(k, j)
                    both = u * scaled
                    gain_acc[j, k] += jnp.sum(both.reshape(rows // 8, 8, kc), axis=0)
                    fresh = fresh + both * gain[k, j]
                mean_acc[...] = fresh

        loop(nk + 1, step)
        mean = jnp.sum(mean_acc[...], axis=-1, keepdims=True) / width

        def finish(k):
            for j in range(nd):
                u, scaled = terms(k, j)
                wide = inverse[t] * (u * gain[k, j] - scaled * mean)
                yret_in[1, k, j] = (grad_ref[k, j].astype(F32) + wide).astype(BF16)
            if t == 1:
                send(yret_in.at[1, k], grad0.at[k], z_s.at[1, k], z_r.at[1, k], pipe=p_down)
            else:
                for j in range(nd):
                    cols = pl.ds(pl.multiple_of(j * quarter + k * kc, kc), kc)
                    pltpu.make_async_copy(yret_in.at[1, k, j], grad_tok.at[:, cols], store_sem.at[1]).start()

        loop(nk, finish)
        settle_return(ph)

    def weight_grads(k):
        both = jnp.zeros((kc, 2 * hidden), F32)
        for t in range(PASSES):
            both = both + lax.dot_general(
                xin[t, k], gate_up[t], (((0,), (0,)), ((), ())), preferred_element_type=F32
            )
        wgu[at(k, kc), :] = both.astype(BF16)
        pltpu.make_async_copy(wgu.at[at(k, kc), 0:hidden], gg.at[at(k, kc)], store_sem.at[2]).start()
        pltpu.make_async_copy(wgu.at[at(k, kc), hidden : 2 * hidden], gu.at[at(k, kc)], store_sem.at[2]).start()
        down = jnp.zeros((hidden, kc), F32)
        for t, ph in ((0, 3), (1, 2)):
            down = down + jnp.dot(act_t[t], xin[ph, k], preferred_element_type=F32)
        wdc[k] = down.astype(BF16)
        pltpu.make_async_copy(wdc.at[k], gd.at[:, at(k, kc)], store_sem.at[3]).start()

    def early0():
        build_places()
        drain(wgu, load_sem.at[1])
        drain(wdc, load_sem.at[2])

    gain_acc[...] = jnp.zeros_like(gain_acc)
    dispatch(0, 0, 0, norm, forward_chunk, early=early0)
    forward_expert(0, 0)
    forward_return(0, 0, tokc)
    drain(cotc, load_sem.at[3])

    dispatch(2, 1, 1, cotc, backward_chunk)
    sum_b = all_sum(2, rs_b, grad_act, one_b, two_b, hidden)
    for g in range(2):
        round_into(rs_b, hidden, g)
        sum_b[0](g)

    def arrived(k, c):
        drain(hid1.at[k], z_r.at[0, k])
        return squares(hid1, k, c)

    normalize(1, hid1, lax.fori_loop(0, nk, arrived, none))
    loop(nk, lambda k: drain(yret_in.at[0, k], z_s.at[0, k]))

    def early1():
        for g in range(2):
            sum_b[1](g)
        for g in range(2):
            sum_b[2](g)
        for g in range(2):
            sum_b[3](g)

    dispatch(1, 0, 1, norm, forward_chunk, early=early1)
    forward_expert(1, 1)
    for g in range(2):
        sum_b[4](g)
    sum_b[5]()
    forward_return(1, 1, hid1)

    backward_expert(2, 1)
    backward_return(2, 1, hid1, cotc, lambda k: None)

    def arrive0(k):
        drain(grad0.at[k], z_r.at[1, k])

    dispatch(3, 1, 0, grad0, backward_chunk, arrive=arrive0)
    loop(nk, lambda k: drain(yret_in.at[1, k], z_s.at[1, k]))
    sum_b = all_sum(3, rs_b, grad_act, one_b, two_b, hidden)
    for g in range(2):
        round_into(rs_b, hidden, g)
        sum_b[0](g)
    for stage in (1, 2, 3, 4):
        for g in range(2):
            sum_b[stage](g)
    sum_b[5]()
    backward_expert(3, 0)
    backward_return(3, 0, tokc, grad0, weight_grads)

    for d in range(1, nd):
        j = lax.rem(q + d, nd)
        send(gain_acc.at[j], gain_dp.at[q], gain_s.at[0], gain_r.at[0], dp=j)
    gain_dp[q] = gain_acc[q]
    drain(gain_dp.at[0 : nd - 1], gain_r.at[0])
    mine = gain_dp[0]
    for j in range(1, nd):
        mine = mine + gain_dp[j]
    gain_ex[e] = mine
    for d in range(1, ne):
        send(gain_ex.at[e], gain_ex.at[e], gain_s.at[1], gain_r.at[1], expert=lax.rem(e + d, ne))
    drain(gain_ex.at[0 : ne - 1], gain_r.at[1])
    mine = gain_ex[0]
    for j in range(1, ne):
        mine = mine + gain_ex[j]
    gain_all[q] = mine
    for d in range(1, nd):
        send(gain_all.at[q], gain_all.at[q], gain_s.at[2], gain_r.at[2], dp=lax.rem(q + d, nd))
    drain(gain_all.at[0 : nd - 1], gain_r.at[2])
    gain_out[...] = jnp.broadcast_to(jnp.sum(gain_all[...], axis=2, keepdims=True), gain_out.shape)

    drain(gain_dp.at[0 : nd - 1], gain_s.at[0])
    drain(gain_ex.at[0 : ne - 1], gain_s.at[1])
    drain(gain_all.at[0 : nd - 1], gain_s.at[2])
    drain(dest_all.at[0 : nd - 1], dest_s)
    drain(yret_in.at[0], store_sem.at[0])
    drain(yret_in.at[1], store_sem.at[1])
    drain(wgu, store_sem.at[2])
    drain(wdc, store_sem.at[3])


def slot_rows(route_now, expert_count, dp_index, dp_count):
    tile_count = route_now.shape[0]
    order = jnp.arange(tile_count, dtype=jnp.int32)
    same = (route_now[:, None] == route_now[None, :]) & (order[None, :] < order[:, None])
    rank = jnp.sum(same.astype(jnp.int32), axis=1)
    first = (route_now * dp_count + dp_index) * (CAP * TILE) + rank * TILE
    return (first[:, None] + jnp.arange(TILE, dtype=jnp.int32)[None, :]).reshape(-1)


def body(tokens, cotangent, gain, w_gate, w_up, w_down, route):
    npipe, nd, ne = lax.axis_size("pipe"), lax.axis_size("dp"), lax.axis_size("expert")
    section = lax.axis_index("pipe")
    rows, width = tokens.shape[1:]
    quarter, hidden = w_gate.shape[2:]
    kc = min(WIDTH, quarter)
    nk = quarter // kc
    block = nd * CAP * TILE
    total = ne * block
    group = total // 2
    half = group // nd // 2
    table = route[0, :, :, 0]
    dest = []
    for t in range(PASSES):
        micro = (section - t + npipe) % npipe
        now = lax.dynamic_index_in_dim(table, micro, 0, keepdims=False)
        dest.append(slot_rows(now, ne, lax.axis_index("dp"), nd).astype(F32))
    dest = jnp.broadcast_to(jnp.stack(dest)[:, None, :], (PASSES, 8, rows))
    gain_chunks = gain[0].reshape(nd, nk, 1, kc).swapaxes(0, 1)

    hbm = pl.BlockSpec(memory_space=pl.ANY)
    vmem = pl.BlockSpec(memory_space=pltpu.VMEM)
    V = pltpu.VMEM
    S = pltpu.SemaphoreType.DMA
    chunks = (nk, nd, rows, kc)
    results = pl.pallas_call(
        functools.partial(kernel, (nd, npipe, ne, rows, width, hidden)),
        out_shape=(
            jax.ShapeDtypeStruct((rows, width), BF16),
            jax.ShapeDtypeStruct((rows, width), BF16),
            jax.ShapeDtypeStruct((nd, nk, 8, kc), F32),
            jax.ShapeDtypeStruct((quarter, hidden), BF16),
            jax.ShapeDtypeStruct((quarter, hidden), BF16),
            jax.ShapeDtypeStruct((hidden, quarter), BF16),
        ),
        in_specs=[vmem, hbm, hbm, vmem, hbm, hbm, hbm],
        out_specs=(hbm, hbm, vmem, hbm, hbm, hbm),
        scratch_shapes=[
            V(chunks, BF16),
            V(chunks, BF16),
            V(chunks, BF16),
            V(chunks, BF16),
            V(chunks, BF16),
            V((quarter, 2 * hidden), BF16),
            V((nk, hidden, kc), BF16),
            V((nd, PASSES, 8, rows), F32),
            V((PASSES, total, nd * rows), BF16),
            V((PASSES, nd * rows, total), BF16),
            V((2, nk, nd * rows, kc), BF16),
            V((nk, total, kc), BF16),
            V((4, nk, total, kc), BF16),
            V((total, 2 * hidden), F32),
            V((PASSES, total, 2 * hidden), BF16),
            V((total, hidden), BF16),
            V((PASSES, hidden, total), BF16),
            V((total, hidden), BF16),
            V((total, 2 * hidden), BF16),
            V((total, hidden), BF16),
            V((2, 2, half, 2 * hidden), BF16),
            V((2, 2, half, hidden), BF16),
            V((2, 2, 2, half, 2 * hidden), BF16),
            V((2, 2, 2, half, hidden), BF16),
            V((nk, total, kc), BF16),
            V((2, nk, total, kc), BF16),
            V((nk, nd * rows, kc), BF16),
            V((2,) + chunks, BF16),
            V((PASSES, rows, 1), F32),
            V((rows, kc), F32),
            V((nd, nk, 8, kc), F32),
            V((nd, nk, 8, kc), F32),
            V((ne, nk, 8, kc), F32),
            V((nd, nk, 8, kc), F32),
            S((4,)),
            S((4,)),
            S(()),
            S(()),
            S((4, nk)),
            S((4, nk)),
            S((4, nk)),
            S((4, nk)),
            S((4, nk)),
            S((4, nk)),
            S((4, nk)),
            S((4, nk)),
            S((2, nk)),
            S((2, nk)),
            S((4, 2, 12)),
            S((4, 2, 2)),
            S((4, 2, 2, 2)),
            S((4, 2, 3, 2)),
            S((3,)),
            S((3,)),
        ],
        compiler_params=pltpu.CompilerParams(
            collective_id=0, has_side_effects=True, vmem_limit_bytes=63_000_000
        ),
        cost_estimate=pl.CostEstimate(
            flops=36 * total * quarter * hidden, bytes_accessed=17 * 2**20, transcendentals=2 * total * hidden
        ),
    )(dest, tokens[0], cotangent[0], gain_chunks, w_gate[0, 0], w_up[0, 0], w_down[0, 0])
    out_rows, entry_grad, gain_total, grad_gate, grad_up, grad_down = results
    return (
        out_rows[None],
        entry_grad[None],
        gain_total[:, :, 0, :].reshape(1, width),
        grad_gate[None, None],
        grad_up[None, None],
        grad_down[None, None],
    )


def solution(mesh):
    placed = (
        P("pipe", ("dp", "expert"), None),
        P("pipe", ("dp", "expert"), None),
        P("pipe", None),
        P("pipe", "expert", "dp", None),
        P("pipe", "expert", "dp", None),
        P("pipe", "expert", None, "dp"),
        P("pipe", None, ("dp", "expert"), None),
    )
    return jax.shard_map(
        body,
        mesh=mesh,
        in_specs=placed,
        out_specs=(
            P("pipe", ("dp", "expert"), None),
            P("pipe", ("dp", "expert"), None),
            P("pipe", None),
            P("pipe", "expert", "dp", None),
            P("pipe", "expert", "dp", None),
            P("pipe", "expert", None, "dp"),
        ),
        check_vma=False,
    )
```

```python
import functools
import math

import jax
import jax.numpy as jnp
from jax import lax
from jax.experimental import pallas as pl
from jax.experimental.pallas import tpu as pltpu
from jax.sharding import PartitionSpec as P

TILE = 8
CAP = 3
PASSES = 2
WIDTH = 256
epsilon = 1e-06
F32 = jnp.float32
BF16 = jnp.bfloat16


def kernel(
    sizes,
    dest, tok, cot, gain, wg, wu, wd,
    out_tok, grad_tok, gain_out, gg, gu, gd,
    tokc, cotc, hid1, grad0, norm, wgu, wdc, dest_own, dest_all, place, back,
    yin, xout, xin, acc, gate_up, act, act_t, grad_act,
    rs_f, rs_b, one_f, one_b, two_f, two_b,
    ret_out, ret_in, yret_out, yret_in, inverse, mean_acc, gain_acc, gain_dp, gain_ex, gain_all,
    load_sem, store_sem, dest_s, dest_r, y_s, y_r, x_s, x_r, rx_s, rx_r, ry_s, ry_r,
    z_s, z_r, ar_s, one_r, two_r, ag_r, gain_s, gain_r,
):
    nd, npipe, ne, rows, width, hidden = sizes
    quarter = width // nd
    kc = min(WIDTH, quarter)
    nk = quarter // kc
    block = nd * CAP * TILE
    total = ne * block
    unit = nd * TILE
    lanes = ((0, unit), (ne * unit, (CAP - 1) * unit))
    q, p, e = lax.axis_index("dp"), lax.axis_index("pipe"), lax.axis_index("expert")
    q_up, q_down, q_far = lax.rem(q + 1, nd), lax.rem(q + nd - 1, nd), lax.rem(q + 2, nd)
    p_up, p_down = lax.rem(p + 1, npipe), lax.rem(p + npipe - 1, npipe)

    def send(src, dst, ssem, rsem, **where):
        pltpu.make_async_remote_copy(
            src_ref=src, dst_ref=dst, send_sem=ssem, recv_sem=rsem,
            device_id=where, device_id_type=pl.DeviceIdType.MESH,
        ).start()

    def drain(ref, sem):
        pltpu.make_async_copy(ref, ref, sem).wait()

    def loop(count, step):
        lax.fori_loop(0, count, lambda i, c: (step(i), c)[1], 0)

    def at(i, size):
        return pl.ds(pl.multiple_of(i * size, size), size)

    def rows_of(g, i):
        base, size = lanes[g]
        return pl.ds(pl.multiple_of(base + i * size, unit), size)

    def span_of(g):
        base, size = lanes[g]
        return slice(base, base + ne * size)

    def gain_of(k, j):
        return gain[0:1, pl.ds(pl.multiple_of(j * quarter + k * kc, kc), kc)]

    for k in range(nk):
        for j in range(nd):
            cols = pl.ds(j * quarter + k * kc, kc)
            pltpu.make_async_copy(tok.at[:, cols], tokc.at[k, j], load_sem.at[0]).start()
    pltpu.make_async_copy(wg, wgu.at[:, 0:hidden], load_sem.at[1]).start()
    pltpu.make_async_copy(wu, wgu.at[:, hidden : 2 * hidden], load_sem.at[1]).start()
    for k in range(nk):
        pltpu.make_async_copy(wd.at[:, pl.ds(k * kc, kc)], wdc.at[k], load_sem.at[2]).start()
    for k in range(nk):
        for j in range(nd):
            cols = pl.ds(j * quarter + k * kc, kc)
            pltpu.make_async_copy(cot.at[:, cols], cotc.at[k, j], load_sem.at[3]).start()

    barrier = pltpu.get_barrier_semaphore()

    def greet(**where):
        pl.semaphore_signal(barrier, inc=1, device_id=where, device_id_type=pl.DeviceIdType.MESH)

    for d in range(1, nd):
        greet(dp=lax.rem(q + d, nd))
    for d in range(1, ne):
        greet(expert=lax.rem(e + d, ne))
    greet(pipe=p_up)
    greet(pipe=p_down)

    drain(tokc, load_sem.at[0])

    def squares(ref, k, before):
        for j in range(nd):
            wide = ref[k, j].astype(F32)
            before = before + jnp.sum(wide * wide, axis=-1, keepdims=True)
        return before

    def normalize(t, ref, total_squares):
        inverse[t] = lax.rsqrt(total_squares / width + epsilon)

        def step(k):
            for j in range(nd):
                norm[k, j] = (ref[k, j].astype(F32) * inverse[t] * gain_of(k, j)).astype(BF16)

        loop(nk, step)

    none = jnp.zeros((rows, 1), F32)
    normalize(0, tokc, lax.fori_loop(0, nk, lambda k, c: squares(tokc, k, c), none))
    pl.semaphore_wait(barrier, nd - 1 + ne - 1 + 2)

    row_tile = lax.broadcasted_iota(jnp.int32, (rows, rows), 1) // TILE
    row_at = lax.broadcasted_iota(jnp.int32, (1, rows), 1)
    earlier = (row_tile.T < row_tile)
    for t in range(PASSES):
        expert_of = jnp.broadcast_to(dest[t, 0:1, :], (rows, rows))
        same = jnp.where(earlier & (expert_of.T == expert_of), 1.0, 0.0).astype(F32)
        rank = jnp.sum(same, axis=0, keepdims=True) / TILE
        inner = (q * TILE + row_at % TILE).astype(F32)
        mine = dest[t, 0:1, :]
        first = mine * unit + inner
        other = ne * unit + mine * ((CAP - 1) * unit) + (rank - 1.0) * unit + inner
        dest_own[t] = jnp.broadcast_to(jnp.where(rank < 0.5, first, other), (8, rows))
    for d in range(1, nd):
        send(dest_own, dest_all.at[q], dest_s, dest_r, dp=lax.rem(q + d, nd))
    dest_all[q] = dest_own[...]

    def build_places():
        drain(dest_all.at[0 : nd - 1], dest_r)
        slot_ids = lax.broadcasted_iota(jnp.int32, (total, rows), 0).astype(F32)
        for t in range(PASSES):
            for s in range(nd):
                hot = jnp.where(slot_ids == dest_all[s, t, 0:1, :], 1.0, 0.0).astype(F32)
                place[t, :, s * rows : (s + 1) * rows] = hot.astype(BF16)
                back[t, s * rows : (s + 1) * rows, :] = hot.T.astype(BF16)


    def y_send(ph, st, src, k):
        for d in range(1, nd):
            j = lax.rem(q + d, nd)
            send(src.at[k, j], yin.at[st, k, at(q, rows)], y_s.at[ph, k], y_r.at[ph, k], dp=j)
        yin[st, k, at(q, rows), :] = src[k, q]

    def y_wait(ph, st, k):
        drain(yin.at[st, k, 0 : (nd - 1) * rows], y_r.at[ph, k])

    def x_send(ph, st, t, k, g):
        def some(m):
            there = at(m, ne * unit)
            xout[k, there, :] = jnp.dot(place[t, there, :], yin[st, k], preferred_element_type=F32).astype(BF16)

        if g == 0:
            some(0)
        else:
            lax.fori_loop(1, CAP, lambda m, c: (some(m), c)[1], 0)
        for d in range(1, ne):
            o = lax.rem(e + d, ne)
            send(xout.at[k, rows_of(g, o)], xin.at[ph, k, rows_of(g, e)], x_s.at[ph, k, g], x_r.at[ph, k, g], expert=o)
        xin[ph, k, rows_of(g, e), :] = xout[k, rows_of(g, e), :]

    def x_wait(ph, k, g):
        drain(xin.at[ph, k, 0 : (ne - 1) * lanes[g][1]], x_r.at[ph, k, g])

    def over_lane(g, step):
        base, size = lanes[g]
        first = base // (ne * unit)
        lax.fori_loop(first, first + size // unit, lambda m, c: (step(at(m, ne * unit)), c)[1], 0)

    def forward_chunk(ph, k, g):
        x_wait(ph, k, g)

        def some(there):
            acc[there, :] += jnp.dot(xin[ph, k, there, :], wgu[at(k, kc), :], preferred_element_type=F32)

        over_lane(g, some)

    def backward_chunk(ph, k, g):
        x_wait(ph, k, g)

        def some(there):
            acc[there, 0:hidden] += lax.dot_general(
                xin[ph, k, there, :], wdc[k], (((1,), (1,)), ((), ())), preferred_element_type=F32
            )

        over_lane(g, some)

    def settle_y(ph, st):
        loop(nk, lambda k: drain(yin.at[st, k, 0 : (nd - 1) * rows], y_s.at[ph, k]))

    def settle_x(ph):
        def step(k):
            for g in range(2):
                drain(xout.at[k, 0 : (ne - 1) * lanes[g][1]], x_s.at[ph, k, g])

        loop(nk, step)

    def all_sum(ph, src, dst, one, two, columns):
        def half_of(g):
            return ne * lanes[g][1] // nd // 2

        def span(g, b, h):
            half = half_of(g)
            return pl.ds(pl.multiple_of(lanes[g][0] + (2 * b + h) * half, half), half)

        def cut(ref, g):
            return ref.at[0 : half_of(g)]

        def open_(g):
            send(src.at[span(g, q_far, 0)], cut(one.at[g, 0], g), ar_s.at[ph, g, 0], one_r.at[ph, g, 0], dp=q_down)
            send(src.at[span(g, q_far, 1)], cut(one.at[g, 1], g), ar_s.at[ph, g, 1], one_r.at[ph, g, 1], dp=q_up)
            send(src.at[span(g, q_down, 1)], cut(two.at[g, 0, 1], g), ar_s.at[ph, g, 2], two_r.at[ph, g, 0, 1], dp=q_down)
            send(src.at[span(g, q_up, 0)], cut(two.at[g, 1, 0], g), ar_s.at[ph, g, 3], two_r.at[ph, g, 1, 0], dp=q_up)

        def middle(g):
            half = half_of(g)
            for side, b in ((0, q_down), (1, q_up)):
                drain(cut(one.at[g, side], g), one_r.at[ph, g, side])
                there = span(g, b, side)
                src[there, :] = (src[there, :].astype(F32) + one[g, side, 0:half].astype(F32)).astype(BF16)
                send(src.at[there], cut(two.at[g, side, side], g), ar_s.at[ph, g, 4 + side], two_r.at[ph, g, side, side], dp=b)

        def own(g):
            half = half_of(g)
            for h in range(2):
                for side in range(2):
                    drain(cut(two.at[g, side, h], g), two_r.at[ph, g, side, h])
                mine = span(g, q, h)
                dst[mine, :] = (
                    src[mine, :].astype(F32) + two[g, 0, h, 0:half].astype(F32) + two[g, 1, h, 0:half].astype(F32)
                ).astype(BF16)
            for i in range(2):
                up, down = span(g, q, i), span(g, q, 1 - i)
                send(dst.at[up], dst.at[up], ar_s.at[ph, g, 6 + i], ag_r.at[ph, g, 0, i], dp=q_up)
                send(dst.at[down], dst.at[down], ar_s.at[ph, g, 8 + i], ag_r.at[ph, g, 1, 1 - i], dp=q_down)

        def pass_on(g):
            first, second = span(g, q_down, 0), span(g, q_up, 1)
            drain(dst.at[first], ag_r.at[ph, g, 0, 0])
            send(dst.at[first], dst.at[first], ar_s.at[ph, g, 10], ag_r.at[ph, g, 2, 0], dp=q_up)
            drain(dst.at[second], ag_r.at[ph, g, 1, 1])
            send(dst.at[second], dst.at[second], ar_s.at[ph, g, 11], ag_r.at[ph, g, 2, 1], dp=q_down)

        def close(g):
            drain(dst.at[span(g, q_down, 1)], ag_r.at[ph, g, 0, 1])
            drain(dst.at[span(g, q_up, 0)], ag_r.at[ph, g, 1, 0])
            drain(dst.at[span(g, q_far, 0)], ag_r.at[ph, g, 2, 0])
            drain(dst.at[span(g, q_far, 1)], ag_r.at[ph, g, 2, 1])

        def settle(g):
            for i in range(12):
                drain(cut(src, g), ar_s.at[ph, g, i])

        return open_, middle, own, pass_on, close, settle

    def small_steps(g, step):
        size = math.gcd(64, ne * unit)
        base, length = lanes[g]
        first = base // size
        lax.fori_loop(first, first + ne * length // size, lambda m, c: (step(at(m, size)), c)[1], 0)

    def round_into(src, columns, g):
        def some(there):
            src[there, :] = acc[there, 0:columns].astype(BF16)

        small_steps(g, some)

    def ret_send(ph, st, g, k):
        for d in range(1, ne):
            o = lax.rem(e + d, ne)
            send(
                ret_out.at[k, rows_of(g, o)], ret_in.at[st, k, rows_of(g, e)],
                rx_s.at[ph, k, g], rx_r.at[ph, k, g], expert=o,
            )
        ret_in[st, k, rows_of(g, e), :] = ret_out[k, rows_of(g, e), :]

    def settle_ret(ph, g):
        loop(nk, lambda k: drain(ret_out.at[k, 0 : (ne - 1) * lanes[g][1]], rx_s.at[ph, k, g]))

    def settle_yret(ph):
        loop(nk, lambda k: drain(yret_out.at[k, 0 : (nd - 1) * rows], ry_s.at[ph, k]))

    short = nd * rows // 2

    def collect(ph, st, t, k):
        for g in range(2):
            drain(ret_in.at[st, k, 0 : (ne - 1) * lanes[g][1]], rx_r.at[ph, k, g])

        def some(m):
            yret_out[k, at(m, short), :] = jnp.dot(
                back[t, at(m, short), :], ret_in[st, k], preferred_element_type=F32
            ).astype(BF16)

        loop(2, some)
        for d in range(1, nd):
            j = lax.rem(q + d, nd)
            send(yret_out.at[k, at(j, rows)], yret_in.at[st, k, q], ry_s.at[ph, k], ry_r.at[ph, k], dp=j)
        yret_in[st, k, q] = yret_out[k, at(q, rows), :]

    def landed(ph, st, k):
        drain(yret_in.at[st, k, 0 : nd - 1], ry_r.at[ph, k])

    def activate(t, g):
        def some(there):
            gate = gate_up[t, there, 0:hidden].astype(F32)
            up = gate_up[t, there, hidden : 2 * hidden].astype(F32)
            act[there, :] = (gate * jax.nn.sigmoid(gate) * up).astype(BF16)

        small_steps(g, some)

    def forward_down(ph, g):
        mine = span_of(g)

        def down(k):
            ret_out[k, mine, :] = jnp.dot(act[mine, :], wdc[k], preferred_element_type=F32).astype(BF16)
            ret_send(ph, 0, g, k)

        loop(nk, down)

    def turn(t):
        wide = math.gcd(total, 128)
        for m in range(total // wide):
            act_t[t, :, m * wide : (m + 1) * wide] = act[m * wide : (m + 1) * wide, :].T

    def before(t, g, with_act):
        def some(there):
            gate = gate_up[t, there, 0:hidden].astype(F32)
            up = gate_up[t, there, hidden : 2 * hidden].astype(F32)
            grad = grad_act[there, :].astype(F32)
            s = jax.nn.sigmoid(gate)
            silu = gate * s
            if with_act:
                act[there, :] = (silu * up).astype(BF16)
            gate_up[t, there, 0:hidden] = (grad * up * s * (1.0 + gate * (1.0 - s))).astype(BF16)
            gate_up[t, there, hidden : 2 * hidden] = (grad * silu).astype(BF16)

        small_steps(g, some)

    def backward_up(ph, t, g):
        mine = span_of(g)

        def up_(k):
            ret_out[k, mine, :] = lax.dot_general(
                gate_up[t, mine, :], wgu[at(k, kc), :], (((1,), (1,)), ((), ())), preferred_element_type=F32
            ).astype(BF16)
            ret_send(ph, 1, g, k)

        loop(nk, up_)

    def to_rows(ref, k, out, sem):
        for j in range(nd):
            cols = pl.ds(pl.multiple_of(j * quarter + k * kc, kc), kc)
            pltpu.make_async_copy(ref.at[k, j], out.at[:, cols], sem).start()

    def add_rows(ph, ref, k):
        landed(ph, 0, k)
        for j in range(nd):
            yret_in[0, k, j] = (ref[k, j].astype(F32) + yret_in[0, k, j].astype(F32)).astype(BF16)

    def terms(t, ref, k, j):
        return yret_in[1, k, j].astype(F32), ref[k, j].astype(F32) * inverse[t]

    def gather_grads(ph, t, ref, k):
        landed(ph, 1, k)
        fresh = mean_acc[...]
        for j in range(nd):
            u, scaled = terms(t, ref, k, j)
            both = u * scaled
            gain_acc[j, k] += jnp.sum(both.reshape(rows // 8, 8, kc), axis=0)
            fresh = fresh + both * gain_of(k, j)
        mean_acc[...] = fresh

    def finish_grads(t, ref, grad_ref, k, mean):
        for j in range(nd):
            u, scaled = terms(t, ref, k, j)
            wide = inverse[t] * (u * gain_of(k, j) - scaled * mean)
            yret_in[1, k, j] = (grad_ref[k, j].astype(F32) + wide).astype(BF16)

    def mean_of():
        return jnp.sum(mean_acc[...], axis=-1, keepdims=True) / width

    def weight_grads(k):
        both = jnp.zeros((kc, 2 * hidden), F32)
        for t in range(PASSES):
            both = both + lax.dot_general(
                xin[t, k], gate_up[t], (((0,), (0,)), ((), ())), preferred_element_type=F32
            )
        wgu[at(k, kc), :] = both.astype(BF16)
        pltpu.make_async_copy(wgu.at[at(k, kc), 0:hidden], gg.at[at(k, kc)], store_sem.at[2]).start()
        pltpu.make_async_copy(wgu.at[at(k, kc), hidden : 2 * hidden], gu.at[at(k, kc)], store_sem.at[2]).start()
        down = jnp.zeros((hidden, kc), F32)
        for t, ph in ((0, 3), (1, 2)):
            down = down + jnp.dot(act_t[t], xin[ph, k], preferred_element_type=F32)
        wdc[k] = down.astype(BF16)
        pltpu.make_async_copy(wdc.at[k], gd.at[:, at(k, kc)], store_sem.at[3]).start()

    lag = 2

    def when(test, step):
        @pl.when(test)
        def _():
            step()

    def forward_to_sums(ph, st, t, sums):
        open_, middle, own, pass_on, close, settle = sums
        acc[...] = jnp.zeros_like(acc)

        def step(i):
            def first():
                y_wait(ph, st, i)
                x_send(ph, st, t, i, 0)

            when(i < nk, first)
            when(i >= lag, lambda: x_send(ph, st, t, i - lag, 1))
            when(i >= 1, lambda: forward_chunk(ph, i - 1, 0))
            when(i >= lag + 1, lambda: forward_chunk(ph, i - lag - 1, 1))

        loop(nk + 1, step)
        round_into(rs_f, 2 * hidden, 0)
        open_(0)
        for k in range(nk + 1 - lag, nk):
            x_send(ph, st, t, k, 1)
        for n, k in enumerate(range(nk - lag, nk)):
            forward_chunk(ph, k, 1)
            if n == 0:
                middle(0)
        own(0)
        round_into(rs_f, 2 * hidden, 1)
        open_(1)
        pass_on(0)
        middle(1)

    gain_acc[...] = jnp.zeros_like(gain_acc)
    loop(nk, lambda k: y_send(0, 0, norm, k))
    build_places()
    drain(wgu, load_sem.at[1])
    drain(wdc, load_sem.at[2])
    drain(cotc, load_sem.at[3])

    sums = all_sum(0, rs_f, gate_up.at[0], one_f, two_f, 2 * hidden)
    forward_to_sums(0, 0, 0, sums)
    sums[4](0)
    activate(0, 0)
    forward_down(0, 0)
    sums[2](1)
    sums[3](1)
    settle_y(0, 0)
    settle_x(0)
    sums[4](1)
    activate(0, 1)
    forward_down(0, 1)
    acc[:, 0:hidden] = jnp.zeros((total, hidden), F32)

    def turn_round(i):
        def first():
            collect(0, 0, 0, i)
            y_send(2, 1, cotc, i)

        def second():
            k = i - 1
            add_rows(0, tokc, k)
            send(yret_in.at[0, k], hid1.at[k], z_s.at[0, k], z_r.at[0, k], pipe=p_up)
            y_wait(2, 1, k)
            x_send(2, 1, 1, k, 0)
            x_send(2, 1, 1, k, 1)

        def third():
            backward_chunk(2, i - 2, 0)
            backward_chunk(2, i - 2, 1)

        when(i < nk, first)
        when((i >= 1) & (i <= nk), second)
        when(i >= 2, third)

    loop(nk + 2, turn_round)
    sums[5](0)
    sums[5](1)
    sums_b = all_sum(2, rs_b, grad_act, one_b, two_b, hidden)
    for g in range(2):
        round_into(rs_b, hidden, g)
        sums_b[0](g)
    turn(0)
    settle_ret(0, 0)
    settle_ret(0, 1)
    settle_yret(0)
    settle_y(2, 1)
    settle_x(2)
    for g in range(2):
        sums_b[1](g)

    def arrived(k, c):
        drain(hid1.at[k], z_r.at[0, k])
        return squares(hid1, k, c)

    so_far = lax.fori_loop(0, nk - 1, arrived, none)
    for g in range(2):
        sums_b[2](g)
    normalize(1, hid1, arrived(nk - 1, so_far))
    loop(nk, lambda k: drain(yret_in.at[0, k], z_s.at[0, k]))

    loop(nk, lambda k: y_send(1, 0, norm, k))
    for g in range(2):
        sums_b[3](g)
    for g in range(2):
        sums_b[4](g)
    sums = all_sum(1, rs_f, gate_up.at[1], one_f, two_f, 2 * hidden)
    forward_to_sums(1, 0, 1, sums)

    sums[4](0)
    sums[5](0)
    before(1, 0, True)
    backward_up(2, 1, 0)
    sums[2](1)
    sums[3](1)
    settle_y(1, 0)
    settle_x(1)
    sums_b[5](0)
    sums_b[5](1)
    sums[4](1)
    sums[5](1)
    before(1, 1, True)
    backward_up(2, 1, 1)
    mean_acc[...] = jnp.zeros_like(mean_acc)

    def back1(i):
        when(i < nk, lambda: collect(2, 1, 1, i))
        when(i >= 1, lambda: gather_grads(2, 1, hid1, i - 1))

    loop(nk + 1, back1)
    mean = mean_of()

    def leave(k):
        finish_grads(1, hid1, cotc, k, mean)
        send(yret_in.at[1, k], grad0.at[k], z_s.at[1, k], z_r.at[1, k], pipe=p_down)

    loop(nk, leave)
    settle_ret(2, 0)
    settle_ret(2, 1)
    settle_yret(2)

    forward_down(1, 0)
    acc[:, 0:hidden] = jnp.zeros((total, hidden), F32)

    def come(i):
        def first():
            drain(grad0.at[i], z_r.at[1, i])
            y_send(3, 1, grad0, i)

        def second():
            y_wait(3, 1, i - 1)
            x_send(3, 1, 0, i - 1, 0)
            x_send(3, 1, 0, i - 1, 1)

        def third():
            backward_chunk(3, i - 2, 0)
            backward_chunk(3, i - 2, 1)

        when(i < nk, first)
        when((i >= 1) & (i <= nk), second)
        when(i >= 2, third)

    loop(nk + 2, come)
    loop(nk, lambda k: drain(yret_in.at[1, k], z_s.at[1, k]))
    sums_b = all_sum(3, rs_b, grad_act, one_b, two_b, hidden)
    for g in range(2):
        round_into(rs_b, hidden, g)
        sums_b[0](g)
    forward_down(1, 1)
    for g in range(2):
        sums_b[1](g)
    sums_b[2](0)
    sums_b[2](1)
    turn(1)
    sums_b[3](0)
    sums_b[3](1)
    settle_ret(1, 0)
    sums_b[4](0)
    before(0, 0, False)
    backward_up(3, 0, 0)
    settle_ret(1, 1)
    sums_b[4](1)
    before(0, 1, False)
    backward_up(3, 0, 1)
    settle_y(3, 1)
    settle_x(3)

    def leave1(i):
        when(i < nk, lambda: collect(1, 0, 1, i))

        def second():
            add_rows(1, hid1, i - 1)
            to_rows(yret_in.at[0], i - 1, out_tok, store_sem.at[0])

        when(i >= 1, second)

    loop(nk + 1, leave1)
    settle_yret(1)
    mean_acc[...] = jnp.zeros_like(mean_acc)

    def back0(i):
        when(i < nk, lambda: collect(3, 1, 0, i))
        when(i >= 1, lambda: gather_grads(3, 0, tokc, i - 1))
        when(i < nk - 1, lambda: weight_grads(i))

    loop(nk + 1, back0)
    for d in range(1, nd):
        j = lax.rem(q + d, nd)
        send(gain_acc.at[j], gain_dp.at[q], gain_s.at[0], gain_r.at[0], dp=j)
    mean = mean_of()

    def last(k):
        finish_grads(0, tokc, grad0, k, mean)
        to_rows(yret_in.at[1], k, grad_tok, store_sem.at[1])

    loop(nk, last)

    gain_dp[q] = gain_acc[q]
    drain(gain_dp.at[0 : nd - 1], gain_r.at[0])
    mine = gain_dp[0]
    for j in range(1, nd):
        mine = mine + gain_dp[j]
    gain_ex[e] = mine
    for d in range(1, ne):
        send(gain_ex.at[e], gain_ex.at[e], gain_s.at[1], gain_r.at[1], expert=lax.rem(e + d, ne))
    weight_grads(nk - 1)
    drain(gain_ex.at[0 : ne - 1], gain_r.at[1])
    mine = gain_ex[0]
    for j in range(1, ne):
        mine = mine + gain_ex[j]
    gain_all[q] = mine
    for d in range(1, nd):
        send(gain_all.at[q], gain_all.at[q], gain_s.at[2], gain_r.at[2], dp=lax.rem(q + d, nd))
    drain(gain_all.at[0 : nd - 1], gain_r.at[2])
    gain_out[...] = jnp.broadcast_to(jnp.sum(gain_all[...], axis=2, keepdims=True), gain_out.shape)

    sums_b[5](0)
    sums_b[5](1)
    settle_ret(3, 0)
    settle_ret(3, 1)
    settle_yret(3)
    drain(gain_dp.at[0 : nd - 1], gain_s.at[0])
    drain(gain_ex.at[0 : ne - 1], gain_s.at[1])
    drain(gain_all.at[0 : nd - 1], gain_s.at[2])
    drain(dest_all.at[0 : nd - 1], dest_s)
    drain(yret_in.at[0], store_sem.at[0])
    drain(yret_in.at[1], store_sem.at[1])
    drain(wgu, store_sem.at[2])
    drain(wdc, store_sem.at[3])


def hand_over(quarter, kc, *refs):
    got, given, sems = refs[0:6], refs[6:12], refs[12]
    copies = []
    for n, i in enumerate((3, 4, 5, 0, 1)):
        size = got[i].shape[0] // 2
        for h in range(2):
            part = pl.ds(h * size, size)
            copies.append(pltpu.make_async_copy(got[i].at[part], given[i].at[part], sems.at[n, h]))
            copies[-1].start()
    for j in range(got[2].shape[0]):
        for k in range(got[2].shape[1]):
            given[2][0:1, j * quarter + k * kc : j * quarter + (k + 1) * kc] = got[2][j, k, 0:1, :]
    for copy in copies:
        copy.wait()


def body(tokens, cotangent, gain, w_gate, w_up, w_down, route):
    npipe, nd, ne = lax.axis_size("pipe"), lax.axis_size("dp"), lax.axis_size("expert")
    section = lax.axis_index("pipe")
    rows, width = tokens.shape[1:]
    quarter, hidden = w_gate.shape[2:]
    kc = min(WIDTH, quarter)
    nk = quarter // kc
    block = nd * CAP * TILE
    total = ne * block
    half = (CAP - 1) * total // CAP // nd // 2
    table = route[0, :, :, 0]
    dest = []
    for t in range(PASSES):
        micro = (section - t + npipe) % npipe
        now = lax.dynamic_index_in_dim(table, micro, 0, keepdims=False)
        dest.append(now.astype(F32))
    dest = jnp.broadcast_to(jnp.stack(dest)[:, None, :, None], (PASSES, 8, rows // TILE, TILE))
    dest = dest.reshape(PASSES, 8, rows)

    hbm = pl.BlockSpec(memory_space=pl.ANY)
    vmem = pl.BlockSpec(memory_space=pltpu.VMEM)
    V = pltpu.VMEM
    S = pltpu.SemaphoreType.DMA
    chunks = (nk, nd, rows, kc)
    results = pl.pallas_call(
        functools.partial(kernel, (nd, npipe, ne, rows, width, hidden)),
        out_shape=(
            jax.ShapeDtypeStruct((rows, width), BF16),
            jax.ShapeDtypeStruct((rows, width), BF16),
            jax.ShapeDtypeStruct((nd, nk, 8, kc), F32),
            jax.ShapeDtypeStruct((quarter, hidden), BF16),
            jax.ShapeDtypeStruct((quarter, hidden), BF16),
            jax.ShapeDtypeStruct((hidden, quarter), BF16),
        ),
        in_specs=[vmem, hbm, hbm, vmem, hbm, hbm, hbm],
        out_specs=(hbm, hbm, vmem, hbm, hbm, hbm),
        scratch_shapes=[
            V(chunks, BF16),
            V(chunks, BF16),
            V(chunks, BF16),
            V(chunks, BF16),
            V(chunks, BF16),
            V((quarter, 2 * hidden), BF16),
            V((nk, hidden, kc), BF16),
            V((PASSES, 8, rows), F32),
            V((nd, PASSES, 8, rows), F32),
            V((PASSES, total, nd * rows), BF16),
            V((PASSES, nd * rows, total), BF16),
            V((2, nk, nd * rows, kc), BF16),
            V((nk, total, kc), BF16),
            V((4, nk, total, kc), BF16),
            V((total, 2 * hidden), F32),
            V((PASSES, total, 2 * hidden), BF16),
            V((total, hidden), BF16),
            V((PASSES, hidden, total), BF16),
            V((total, hidden), BF16),
            V((total, 2 * hidden), BF16),
            V((total, hidden), BF16),
            V((2, 2, half, 2 * hidden), BF16),
            V((2, 2, half, hidden), BF16),
            V((2, 2, 2, half, 2 * hidden), BF16),
            V((2, 2, 2, half, hidden), BF16),
            V((nk, total, kc), BF16),
            V((2, nk, total, kc), BF16),
            V((nk, nd * rows, kc), BF16),
            V((2,) + chunks, BF16),
            V((PASSES, rows, 1), F32),
            V((rows, kc), F32),
            V((nd, nk, 8, kc), F32),
            V((nd, nk, 8, kc), F32),
            V((ne, nk, 8, kc), F32),
            V((nd, nk, 8, kc), F32),
            S((4,)),
            S((4,)),
            S(()),
            S(()),
            S((4, nk)),
            S((4, nk)),
            S((4, nk, 2)),
            S((4, nk, 2)),
            S((4, nk, 2)),
            S((4, nk, 2)),
            S((4, nk)),
            S((4, nk)),
            S((2, nk)),
            S((2, nk)),
            S((4, 2, 12)),
            S((4, 2, 2)),
            S((4, 2, 2, 2)),
            S((4, 2, 3, 2)),
            S((3,)),
            S((3,)),
        ],
        compiler_params=pltpu.CompilerParams(
            collective_id=0, has_side_effects=True, vmem_limit_bytes=63_000_000
        ),
        cost_estimate=pl.CostEstimate(
            flops=36 * total * quarter * hidden, bytes_accessed=17 * 2**20, transcendentals=2 * total * hidden
        ),
    )(dest, tokens[0], cotangent[0], gain, w_gate[0, 0], w_up[0, 0], w_down[0, 0])
    out_rows, entry_grad, gain_total, grad_gate, grad_up, grad_down = pl.pallas_call(
        functools.partial(hand_over, quarter, kc),
        out_shape=(
            results[0],
            results[1],
            jax.ShapeDtypeStruct((1, width), F32),
            results[3],
            results[4],
            results[5],
        ),
        in_specs=[hbm, hbm, vmem, hbm, hbm, hbm],
        out_specs=(hbm, hbm, vmem, hbm, hbm, hbm),
        scratch_shapes=[S((5, 2))],
    )(*results)
    return (
        out_rows[None],
        entry_grad[None],
        gain_total,
        grad_gate[None, None],
        grad_up[None, None],
        grad_down[None, None],
    )


def solution(mesh):
    placed = (
        P("pipe", ("dp", "expert"), None),
        P("pipe", ("dp", "expert"), None),
        P("pipe", None),
        P("pipe", "expert", "dp", None),
        P("pipe", "expert", "dp", None),
        P("pipe", "expert", None, "dp"),
        P("pipe", None, ("dp", "expert"), None),
    )
    return jax.shard_map(
        body,
        mesh=mesh,
        in_specs=placed,
        out_specs=(
            P("pipe", ("dp", "expert"), None),
            P("pipe", ("dp", "expert"), None),
            P("pipe", None),
            P("pipe", "expert", "dp", None),
            P("pipe", "expert", "dp", None),
            P("pipe", "expert", None, "dp"),
        ),
        check_vma=False,
    )
```

```python
import functools
import math

import jax
import jax.numpy as jnp
from jax import lax
from jax.experimental import pallas as pl
from jax.experimental.pallas import tpu as pltpu
from jax.sharding import PartitionSpec as P

TILE = 8
CAP = 3
PASSES = 2
WIDTH = 256
epsilon = 1e-06
F32 = jnp.float32
BF16 = jnp.bfloat16


def kernel(
    sizes,
    dest, tok, cot, gain, wg, wu, wd,
    out_tok, grad_tok, gain_out, gg, gu, gd,
    tokc, cotc, hid1, grad0, norm, wgu, wdc, dest_own, dest_all, place, back,
    yin, xout, xin, acc, gate_up, act, act_t, grad_act,
    rs_f, rs_b, one_f, one_b, two_f, two_b,
    ret_out, ret_in, yret_out, yret_in, inverse, mean_acc, gain_acc, gain_dp, gain_ex, gain_all,
    load_sem, store_sem, dest_s, dest_r, y_s, y_r, x_s, x_r, rx_s, rx_r, ry_s, ry_r,
    z_s, z_r, sum_s, one_r, two_r, give_s, give_r, gain_s, gain_r,
):
    nd, npipe, ne, rows, width, hidden = sizes
    quarter = width // nd
    kc = min(WIDTH, quarter)
    nk = quarter // kc
    block = nd * CAP * TILE
    total = ne * block
    unit = nd * TILE
    lane = ne * unit
    lanes = range(CAP)
    half = lane // nd // 2
    q, p, e = lax.axis_index("dp"), lax.axis_index("pipe"), lax.axis_index("expert")
    q_up, q_down, q_far = lax.rem(q + 1, nd), lax.rem(q + nd - 1, nd), lax.rem(q + 2, nd)
    p_up, p_down = lax.rem(p + 1, npipe), lax.rem(p + npipe - 1, npipe)

    def send(src, dst, ssem, rsem, **where):
        pltpu.make_async_remote_copy(
            src_ref=src, dst_ref=dst, send_sem=ssem, recv_sem=rsem,
            device_id=where, device_id_type=pl.DeviceIdType.MESH,
        ).start()

    def drain(ref, sem):
        pltpu.make_async_copy(ref, ref, sem).wait()

    def loop(count, step):
        lax.fori_loop(0, count, lambda i, c: (step(i), c)[1], 0)

    def at(i, size):
        return pl.ds(pl.multiple_of(i * size, size), size)

    def rows_of(g, i):
        return pl.ds(pl.multiple_of(g * lane + i * unit, unit), unit)

    def span_of(g):
        return slice(g * lane, (g + 1) * lane)

    def gain_of(k, j):
        return gain[0:1, pl.ds(pl.multiple_of(j * quarter + k * kc, kc), kc)]

    for k in range(nk):
        for j in range(nd):
            cols = pl.ds(j * quarter + k * kc, kc)
            pltpu.make_async_copy(tok.at[:, cols], tokc.at[k, j], load_sem.at[0]).start()
    pltpu.make_async_copy(wg, wgu.at[:, 0:hidden], load_sem.at[1]).start()
    pltpu.make_async_copy(wu, wgu.at[:, hidden : 2 * hidden], load_sem.at[1]).start()
    for k in range(nk):
        pltpu.make_async_copy(wd.at[:, pl.ds(k * kc, kc)], wdc.at[k], load_sem.at[2]).start()
    for k in range(nk):
        for j in range(nd):
            cols = pl.ds(j * quarter + k * kc, kc)
            pltpu.make_async_copy(cot.at[:, cols], cotc.at[k, j], load_sem.at[3]).start()

    barrier = pltpu.get_barrier_semaphore()

    def greet(**where):
        pl.semaphore_signal(barrier, inc=1, device_id=where, device_id_type=pl.DeviceIdType.MESH)

    for d in range(1, nd):
        greet(dp=lax.rem(q + d, nd))
    for d in range(1, ne):
        greet(expert=lax.rem(e + d, ne))
    greet(pipe=p_up)
    greet(pipe=p_down)

    drain(tokc, load_sem.at[0])

    def squares(ref, k, before):
        for j in range(nd):
            wide = ref[k, j].astype(F32)
            before = before + jnp.sum(wide * wide, axis=-1, keepdims=True)
        return before

    def normalize(t, ref, total_squares):
        inverse[t] = lax.rsqrt(total_squares / width + epsilon)

        def step(k):
            for j in range(nd):
                norm[k, j] = (ref[k, j].astype(F32) * inverse[t] * gain_of(k, j)).astype(BF16)

        loop(nk, step)

    none = jnp.zeros((rows, 1), F32)
    normalize(0, tokc, lax.fori_loop(0, nk, lambda k, c: squares(tokc, k, c), none))
    pl.semaphore_wait(barrier, nd - 1 + ne - 1 + 2)

    row_tile = lax.broadcasted_iota(jnp.int32, (rows, rows), 1) // TILE
    row_at = lax.broadcasted_iota(jnp.int32, (1, rows), 1)
    earlier = (row_tile.T < row_tile)
    for t in range(PASSES):
        expert_of = jnp.broadcast_to(dest[t, 0:1, :], (rows, rows))
        same = jnp.where(earlier & (expert_of.T == expert_of), 1.0, 0.0).astype(F32)
        rank = jnp.sum(same, axis=0, keepdims=True) / TILE
        inner = (q * TILE + row_at % TILE).astype(F32)
        mine = dest[t, 0:1, :]
        dest_own[t] = jnp.broadcast_to(rank * lane + mine * unit + inner, (8, rows))
    for d in range(1, nd):
        send(dest_own, dest_all.at[q], dest_s, dest_r, dp=lax.rem(q + d, nd))
    dest_all[q] = dest_own[...]

    def build_places():
        drain(dest_all.at[0 : nd - 1], dest_r)
        slot_ids = lax.broadcasted_iota(jnp.int32, (total, rows), 0).astype(F32)
        for t in range(PASSES):
            for s in range(nd):
                hot = jnp.where(slot_ids == dest_all[s, t, 0:1, :], 1.0, 0.0).astype(F32)
                place[t, :, s * rows : (s + 1) * rows] = hot.astype(BF16)
                back[t, s * rows : (s + 1) * rows, :] = hot.T.astype(BF16)


    def y_send(ph, st, src, k):
        for d in range(1, nd):
            j = lax.rem(q + d, nd)
            send(src.at[k, j], yin.at[st, k, at(q, rows)], y_s.at[ph, k], y_r.at[ph, k], dp=j)
        yin[st, k, at(q, rows), :] = src[k, q]

    def y_wait(ph, st, k):
        drain(yin.at[st, k, 0 : (nd - 1) * rows], y_r.at[ph, k])

    def x_send(ph, st, t, k, g):
        mine = span_of(g)
        xout[k, mine, :] = jnp.dot(place[t, mine, :], yin[st, k], preferred_element_type=F32).astype(BF16)
        for d in range(1, ne):
            o = lax.rem(e + d, ne)
            send(xout.at[k, rows_of(g, o)], xin.at[ph, k, rows_of(g, e)], x_s.at[ph, k, g], x_r.at[ph, k, g], expert=o)
        xin[ph, k, rows_of(g, e), :] = xout[k, rows_of(g, e), :]

    def x_wait(ph, k, g):
        drain(xin.at[ph, k, 0 : (ne - 1) * unit], x_r.at[ph, k, g])

    def forward_chunk(ph, k, g):
        x_wait(ph, k, g)
        mine = span_of(g)
        acc[mine, :] += jnp.dot(xin[ph, k, mine, :], wgu[at(k, kc), :], preferred_element_type=F32)

    def backward_chunk(ph, k):
        for g in lanes:
            x_wait(ph, k, g)

        def some(m):
            there = at(m, lane)
            acc[there, 0:hidden] += lax.dot_general(
                xin[ph, k, there, :], wdc[k], (((1,), (1,)), ((), ())), preferred_element_type=F32
            )

        loop(CAP, some)

    def settle_y(ph, st):
        loop(nk, lambda k: drain(yin.at[st, k, 0 : (nd - 1) * rows], y_s.at[ph, k]))

    def settle_x(ph):
        def step(k):
            for g in lanes:
                drain(xout.at[k, 0 : (ne - 1) * unit], x_s.at[ph, k, g])

        loop(nk, step)

    def span(g, b, h):
        return pl.ds(pl.multiple_of(g * lane + (2 * b + h) * half, half), half)

    def summing(ph, src, one, two):
        def open_(g):
            send(src.at[span(g, q_far, 0)], one.at[g, 0], sum_s.at[ph, g, 0], one_r.at[ph, g, 0], dp=q_down)
            send(src.at[span(g, q_far, 1)], one.at[g, 1], sum_s.at[ph, g, 1], one_r.at[ph, g, 1], dp=q_up)
            send(src.at[span(g, q_down, 1)], two.at[g, 0, 1], sum_s.at[ph, g, 2], two_r.at[ph, g, 0, 1], dp=q_down)
            send(src.at[span(g, q_up, 0)], two.at[g, 1, 0], sum_s.at[ph, g, 3], two_r.at[ph, g, 1, 0], dp=q_up)

        def middle(g):
            for side, b in ((0, q_down), (1, q_up)):
                drain(one.at[g, side], one_r.at[ph, g, side])
                there = span(g, b, side)
                src[there, :] = (src[there, :].astype(F32) + one[g, side].astype(F32)).astype(BF16)
                send(src.at[there], two.at[g, side, side], sum_s.at[ph, g, 4 + side], two_r.at[ph, g, side, side], dp=b)

        def whole(g, h):
            for side in range(2):
                drain(two.at[g, side, h], two_r.at[ph, g, side, h])
            return src[span(g, q, h), :].astype(F32) + two[g, 0, h].astype(F32) + two[g, 1, h].astype(F32)

        def settle(g):
            for i in range(6):
                drain(src.at[0:half], sum_s.at[ph, g, i])

        return open_, middle, whole, settle

    def giving(ph, dst):
        def offer(g):
            for i in range(2):
                up, down = span(g, q, i), span(g, q, 1 - i)
                send(dst.at[up], dst.at[up], give_s.at[ph, g, i], give_r.at[ph, g, 0, i], dp=q_up)
                send(dst.at[down], dst.at[down], give_s.at[ph, g, 2 + i], give_r.at[ph, g, 1, 1 - i], dp=q_down)

        def pass_on(g):
            first, second = span(g, q_down, 0), span(g, q_up, 1)
            drain(dst.at[first], give_r.at[ph, g, 0, 0])
            send(dst.at[first], dst.at[first], give_s.at[ph, g, 4], give_r.at[ph, g, 2, 0], dp=q_up)
            drain(dst.at[second], give_r.at[ph, g, 1, 1])
            send(dst.at[second], dst.at[second], give_s.at[ph, g, 5], give_r.at[ph, g, 2, 1], dp=q_down)

        def close(g):
            drain(dst.at[span(g, q_down, 1)], give_r.at[ph, g, 0, 1])
            drain(dst.at[span(g, q_up, 0)], give_r.at[ph, g, 1, 0])
            drain(dst.at[span(g, q_far, 0)], give_r.at[ph, g, 2, 0])
            drain(dst.at[span(g, q_far, 1)], give_r.at[ph, g, 2, 1])

        def settle(g):
            for i in range(6):
                drain(dst.at[0:half], give_s.at[ph, g, i])

        return offer, pass_on, close, settle

    def small_steps(g, step):
        size = math.gcd(64, lane)
        lax.fori_loop(g * (lane // size), (g + 1) * (lane // size), lambda m, c: (step(at(m, size)), c)[1], 0)

    def round_into(src, columns, g):
        def some(there):
            src[there, :] = acc[there, 0:columns].astype(BF16)

        small_steps(g, some)

    def ret_send(ph, st, g, k):
        for d in range(1, ne):
            o = lax.rem(e + d, ne)
            send(
                ret_out.at[k, rows_of(g, o)], ret_in.at[st, k, rows_of(g, e)],
                rx_s.at[ph, k, g], rx_r.at[ph, k, g], expert=o,
            )
        ret_in[st, k, rows_of(g, e), :] = ret_out[k, rows_of(g, e), :]

    def settle_ret(ph, g):
        loop(nk, lambda k: drain(ret_out.at[k, 0 : (ne - 1) * unit], rx_s.at[ph, k, g]))

    def settle_yret(ph):
        loop(nk, lambda k: drain(yret_out.at[k, 0 : (nd - 1) * rows], ry_s.at[ph, k]))

    short = nd * rows // 2

    def collect(ph, st, t, k):
        for g in lanes:
            drain(ret_in.at[st, k, 0 : (ne - 1) * unit], rx_r.at[ph, k, g])

        def some(m):
            yret_out[k, at(m, short), :] = jnp.dot(
                back[t, at(m, short), :], ret_in[st, k], preferred_element_type=F32
            ).astype(BF16)

        loop(2, some)
        for d in range(1, nd):
            j = lax.rem(q + d, nd)
            send(yret_out.at[k, at(j, rows)], yret_in.at[st, k, q], ry_s.at[ph, k], ry_r.at[ph, k], dp=j)
        yret_in[st, k, q] = yret_out[k, at(q, rows), :]

    def landed(ph, st, k):
        drain(yret_in.at[st, k, 0 : nd - 1], ry_r.at[ph, k])

    def activate(t, g):
        def some(there):
            gate = gate_up[t, there, 0:hidden].astype(F32)
            up = gate_up[t, there, hidden : 2 * hidden].astype(F32)
            act[there, :] = (gate * jax.nn.sigmoid(gate) * up).astype(BF16)

        small_steps(g, some)

    def forward_down(ph, g, beside=None):
        mine = span_of(g)

        def down(k):
            ret_out[k, mine, :] = jnp.dot(act[mine, :], wdc[k], preferred_element_type=F32).astype(BF16)
            ret_send(ph, 0, g, k)
            if beside is not None:
                beside(k)

        loop(nk, down)

    def turn(t):
        wide = math.gcd(total, 128)
        for m in range(total // wide):
            act_t[t, :, m * wide : (m + 1) * wide] = act[m * wide : (m + 1) * wide, :].T

    def pre_grads(gate, up, grad):
        s = jax.nn.sigmoid(gate)
        silu = gate * s
        return grad * up * s * (1.0 + gate * (1.0 - s)), grad * silu, silu * up

    def before(t, g):
        def some(there):
            gate = gate_up[t, there, 0:hidden].astype(F32)
            up = gate_up[t, there, hidden : 2 * hidden].astype(F32)
            of_gate, of_up, _ = pre_grads(gate, up, grad_act[there, :].astype(F32))
            gate_up[t, there, 0:hidden] = of_gate.astype(BF16)
            gate_up[t, there, hidden : 2 * hidden] = of_up.astype(BF16)

        small_steps(g, some)

    def backward_up(ph, t, g):
        mine = span_of(g)

        def up_(k):
            ret_out[k, mine, :] = lax.dot_general(
                gate_up[t, mine, :], wgu[at(k, kc), :], (((1,), (1,)), ((), ())), preferred_element_type=F32
            ).astype(BF16)
            ret_send(ph, 1, g, k)

        loop(nk, up_)

    def to_rows(ref, k, out, sem):
        for j in range(nd):
            cols = pl.ds(pl.multiple_of(j * quarter + k * kc, kc), kc)
            pltpu.make_async_copy(ref.at[k, j], out.at[:, cols], sem).start()

    def add_rows(ph, ref, k):
        landed(ph, 0, k)
        for j in range(nd):
            yret_in[0, k, j] = (ref[k, j].astype(F32) + yret_in[0, k, j].astype(F32)).astype(BF16)

    def terms(t, ref, k, j):
        return yret_in[1, k, j].astype(F32), ref[k, j].astype(F32) * inverse[t]

    def gather_grads(ph, t, ref, k):
        landed(ph, 1, k)
        fresh = mean_acc[...]
        for j in range(nd):
            u, scaled = terms(t, ref, k, j)
            both = u * scaled
            gain_acc[j, k] += jnp.sum(both.reshape(rows // 8, 8, kc), axis=0)
            fresh = fresh + both * gain_of(k, j)
        mean_acc[...] = fresh

    def finish_grads(t, ref, grad_ref, k, mean):
        for j in range(nd):
            u, scaled = terms(t, ref, k, j)
            wide = inverse[t] * (u * gain_of(k, j) - scaled * mean)
            yret_in[1, k, j] = (grad_ref[k, j].astype(F32) + wide).astype(BF16)

    def mean_of():
        return jnp.sum(mean_acc[...], axis=-1, keepdims=True) / width

    def weight_grads(k):
        both = jnp.zeros((kc, 2 * hidden), F32)
        for t in range(PASSES):
            both = both + lax.dot_general(
                xin[t, k], gate_up[t], (((0,), (0,)), ((), ())), preferred_element_type=F32
            )
        wgu[at(k, kc), :] = both.astype(BF16)
        pltpu.make_async_copy(wgu.at[at(k, kc), 0:hidden], gg.at[at(k, kc)], store_sem.at[2]).start()
        pltpu.make_async_copy(wgu.at[at(k, kc), hidden : 2 * hidden], gu.at[at(k, kc)], store_sem.at[2]).start()
        down = jnp.zeros((hidden, kc), F32)
        for t, ph in ((0, 3), (1, 2)):
            down = down + jnp.dot(act_t[t], xin[ph, k], preferred_element_type=F32)
        wdc[k] = down.astype(BF16)
        pltpu.make_async_copy(wdc.at[k], gd.at[:, at(k, kc)], store_sem.at[3]).start()

    def when(test, step):
        @pl.when(test)
        def _():
            step()

    lag = 2

    def forward_to_sums(ph, st, t, sums, mine, gives):
        open_, middle = sums[0], sums[1]
        acc[...] = jnp.zeros_like(acc)

        def step(i):
            for g in lanes:
                def first(g=g):
                    if g == 0:
                        y_wait(ph, st, i)
                    x_send(ph, st, t, i - g * lag, g)

                when((i >= g * lag) & (i < nk + g * lag), first)
            for g in lanes:
                when((i >= g * lag + 1) & (i < nk + g * lag + 1), lambda g=g: forward_chunk(ph, i - g * lag - 1, g))

        def start(g):
            round_into(rs_f, 2 * hidden, g)
            open_(g)

        def run(first, last):
            lax.fori_loop(first, last, lambda i, c: (step(i), c)[1], 0)

        run(0, nk + 1)
        start(0)
        run(nk + 1, nk + 2)
        middle(0)
        run(nk + 2, nk + 3)
        start(1)
        mine(0)
        run(nk + 3, nk + 4)
        gives[1](0)
        middle(1)
        run(nk + 4, nk + 5)
        start(2)
        mine(1)
        middle(2)

    gain_acc[...] = jnp.zeros_like(gain_acc)
    loop(nk, lambda k: y_send(0, 0, norm, k))
    build_places()
    drain(wgu, load_sem.at[1])
    drain(wdc, load_sem.at[2])
    drain(cotc, load_sem.at[3])

    sums = summing(0, rs_f, one_f, two_f)
    gives = giving(0, gate_up.at[0])

    def mine0(g):
        for h in range(2):
            gate_up[0, span(g, q, h), :] = sums[2](g, h).astype(BF16)
        gives[0](g)

    forward_to_sums(0, 0, 0, sums, mine0, gives)
    gives[2](0)
    activate(0, 0)
    forward_down(0, 0)
    gives[1](1)
    mine0(2)
    settle_y(0, 0)
    settle_x(0)
    gives[2](1)
    activate(0, 1)
    forward_down(0, 1)
    gives[1](2)
    acc[:, 0:hidden] = jnp.zeros((total, hidden), F32)
    gives[2](2)
    activate(0, 2)
    forward_down(0, 2, lambda k: y_send(2, 1, cotc, k))

    def turn_round(i):
        def second():
            k = i - 1
            add_rows(0, tokc, k)
            send(yret_in.at[0, k], hid1.at[k], z_s.at[0, k], z_r.at[0, k], pipe=p_up)
            y_wait(2, 1, k)
            for g in lanes:
                x_send(2, 1, 1, k, g)

        when(i < nk, lambda: collect(0, 0, 0, i))
        when((i >= 1) & (i <= nk), second)
        when(i >= 2, lambda: backward_chunk(2, i - 2))

    loop(nk + 2, turn_round)
    sums_b = summing(2, rs_b, one_b, two_b)
    for g in lanes:
        round_into(rs_b, hidden, g)
        sums_b[0](g)
    turn(0)
    for g in lanes:
        sums[3](g)
        gives[3](g)
        settle_ret(0, g)
    settle_yret(0)
    settle_y(2, 1)
    settle_x(2)

    def arrived(k, c):
        drain(hid1.at[k], z_r.at[0, k])
        return squares(hid1, k, c)

    so_far = lax.fori_loop(0, nk - 1, arrived, none)
    for g in lanes:
        sums_b[1](g)
    normalize(1, hid1, arrived(nk - 1, so_far))
    loop(nk, lambda k: drain(yret_in.at[0, k], z_s.at[0, k]))

    loop(nk, lambda k: y_send(1, 0, norm, k))
    sums = summing(1, rs_f, one_f, two_f)
    gives = giving(1, gate_up.at[1])

    def mine1(g):
        for h in range(2):
            there = span(g, q, h)
            both = sums[2](g, h)
            of_gate, of_up, activated = pre_grads(both[:, 0:hidden], both[:, hidden : 2 * hidden], sums_b[2](g, h))
            gate_up[1, there, 0:hidden] = of_gate.astype(BF16)
            gate_up[1, there, hidden : 2 * hidden] = of_up.astype(BF16)
            act[there, :] = activated.astype(BF16)
        gives[0](g)

    forward_to_sums(1, 0, 1, sums, mine1, gives)

    gives[2](0)
    backward_up(2, 1, 0)
    gives[1](1)
    mine1(2)
    settle_y(1, 0)
    settle_x(1)
    gives[2](1)
    backward_up(2, 1, 1)
    gives[1](2)
    mean_acc[...] = jnp.zeros_like(mean_acc)
    gives[2](2)
    backward_up(2, 1, 2)

    def back1(i):
        when(i < nk, lambda: collect(2, 1, 1, i))
        when(i >= 1, lambda: gather_grads(2, 1, hid1, i - 1))

    loop(nk + 1, back1)
    mean = mean_of()

    def leave(k):
        finish_grads(1, hid1, cotc, k, mean)
        send(yret_in.at[1, k], grad0.at[k], z_s.at[1, k], z_r.at[1, k], pipe=p_down)

    loop(nk, leave)

    acts = giving(4, act)
    for g in lanes:
        acts[0](g)
    for g in lanes:
        sums[3](g)
        gives[3](g)
        sums_b[3](g)
        settle_ret(2, g)
    settle_yret(2)
    acc[:, 0:hidden] = jnp.zeros((total, hidden), F32)

    def come(i):
        def first():
            drain(grad0.at[i], z_r.at[1, i])
            y_send(3, 1, grad0, i)

        def second():
            y_wait(3, 1, i - 1)
            for g in lanes:
                x_send(3, 1, 0, i - 1, g)

        when(i < nk, first)
        when((i >= 1) & (i <= nk), second)
        when(i >= 2, lambda: backward_chunk(3, i - 2))

    loop(1, come)
    for g in lanes:
        acts[1](g)
    for g in lanes:
        acts[2](g)
    forward_down(1, 0)
    turn(1)
    lax.fori_loop(1, nk + 2, lambda i, c: (come(i), c)[1], 0)
    loop(nk, lambda k: drain(yret_in.at[1, k], z_s.at[1, k]))
    sums_b = summing(3, rs_b, one_b, two_b)
    gives = giving(3, grad_act)

    def mine3(g):
        for h in range(2):
            grad_act[span(g, q, h), :] = sums_b[2](g, h).astype(BF16)
        gives[0](g)

    for g in lanes:
        round_into(rs_b, hidden, g)
        sums_b[0](g)
    forward_down(1, 1)
    for g in lanes:
        sums_b[1](g)
    forward_down(1, 2)
    for g in lanes:
        mine3(g)
        if g >= 1:
            gives[1](g - 1)
    gives[1](CAP - 1)
    settle_y(3, 1)
    settle_x(3)
    for g in lanes:
        gives[2](g)
        before(0, g)
        settle_ret(1, g)
        backward_up(3, 0, g)

    def leave1(i):
        when(i < nk, lambda: collect(1, 0, 1, i))

        def second():
            add_rows(1, hid1, i - 1)
            to_rows(yret_in.at[0], i - 1, out_tok, store_sem.at[0])

        when(i >= 1, second)

    loop(nk + 1, leave1)
    settle_yret(1)
    mean_acc[...] = jnp.zeros_like(mean_acc)

    def back0(i):
        when(i < nk, lambda: collect(3, 1, 0, i))
        when(i >= 1, lambda: gather_grads(3, 0, tokc, i - 1))
        when(i < nk - 1, lambda: weight_grads(i))

    loop(nk + 1, back0)
    for d in range(1, nd):
        j = lax.rem(q + d, nd)
        send(gain_acc.at[j], gain_dp.at[q], gain_s.at[0], gain_r.at[0], dp=j)
    mean = mean_of()

    def last(k):
        finish_grads(0, tokc, grad0, k, mean)
        to_rows(yret_in.at[1], k, grad_tok, store_sem.at[1])

    loop(nk, last)

    gain_dp[q] = gain_acc[q]
    drain(gain_dp.at[0 : nd - 1], gain_r.at[0])
    mine = gain_dp[0]
    for j in range(1, nd):
        mine = mine + gain_dp[j]
    gain_ex[e] = mine
    for d in range(1, ne):
        send(gain_ex.at[e], gain_ex.at[e], gain_s.at[1], gain_r.at[1], expert=lax.rem(e + d, ne))
    weight_grads(nk - 1)
    drain(gain_ex.at[0 : ne - 1], gain_r.at[1])
    mine = gain_ex[0]
    for j in range(1, ne):
        mine = mine + gain_ex[j]
    gain_all[q] = mine
    for d in range(1, nd):
        send(gain_all.at[q], gain_all.at[q], gain_s.at[2], gain_r.at[2], dp=lax.rem(q + d, nd))
    drain(gain_all.at[0 : nd - 1], gain_r.at[2])
    gain_out[...] = jnp.broadcast_to(jnp.sum(gain_all[...], axis=2, keepdims=True), gain_out.shape)

    for g in lanes:
        sums_b[3](g)
        gives[3](g)
        acts[3](g)
        settle_ret(3, g)
    settle_yret(3)
    drain(gain_dp.at[0 : nd - 1], gain_s.at[0])
    drain(gain_ex.at[0 : ne - 1], gain_s.at[1])
    drain(gain_all.at[0 : nd - 1], gain_s.at[2])
    drain(dest_all.at[0 : nd - 1], dest_s)
    drain(yret_in.at[0], store_sem.at[0])
    drain(yret_in.at[1], store_sem.at[1])
    drain(wgu, store_sem.at[2])
    drain(wdc, store_sem.at[3])


def hand_over(quarter, kc, *refs):
    got, given, stages, sems = refs[0:6], refs[6:12], refs[12:17], refs[17]
    order = (3, 4, 5, 0, 1)

    def piece(n, h, way):
        size = stages[n].shape[0] // 2
        part = pl.ds(h * size, size)
        ends = (got[order[n]].at[part], stages[n].at[part], given[order[n]].at[part])
        return pltpu.make_async_copy(ends[way], ends[way + 1], sems.at[way, n, h])

    each = [(n, h) for n in range(len(order)) for h in range(2)]
    for n, h in each:
        piece(n, h, 0).start()
    for j in range(got[2].shape[0]):
        for k in range(got[2].shape[1]):
            given[2][0:1, j * quarter + k * kc : j * quarter + (k + 1) * kc] = got[2][j, k, 0:1, :]
    for n, h in each:
        piece(n, h, 0).wait()
        piece(n, h, 1).start()
    for n, h in each:
        piece(n, h, 1).wait()


def body(tokens, cotangent, gain, w_gate, w_up, w_down, route):
    npipe, nd, ne = lax.axis_size("pipe"), lax.axis_size("dp"), lax.axis_size("expert")
    section = lax.axis_index("pipe")
    rows, width = tokens.shape[1:]
    quarter, hidden = w_gate.shape[2:]
    kc = min(WIDTH, quarter)
    nk = quarter // kc
    block = nd * CAP * TILE
    total = ne * block
    half = total // CAP // nd // 2
    table = route[0, :, :, 0]
    dest = []
    for t in range(PASSES):
        micro = (section - t + npipe) % npipe
        now = lax.dynamic_index_in_dim(table, micro, 0, keepdims=False)
        dest.append(now.astype(F32))
    dest = jnp.broadcast_to(jnp.stack(dest)[:, None, :, None], (PASSES, 8, rows // TILE, TILE))
    dest = dest.reshape(PASSES, 8, rows)

    hbm = pl.BlockSpec(memory_space=pl.ANY)
    vmem = pl.BlockSpec(memory_space=pltpu.VMEM)
    V = pltpu.VMEM
    S = pltpu.SemaphoreType.DMA
    chunks = (nk, nd, rows, kc)
    results = pl.pallas_call(
        functools.partial(kernel, (nd, npipe, ne, rows, width, hidden)),
        out_shape=(
            jax.ShapeDtypeStruct((rows, width), BF16),
            jax.ShapeDtypeStruct((rows, width), BF16),
            jax.ShapeDtypeStruct((nd, nk, 8, kc), F32),
            jax.ShapeDtypeStruct((quarter, hidden), BF16),
            jax.ShapeDtypeStruct((quarter, hidden), BF16),
            jax.ShapeDtypeStruct((hidden, quarter), BF16),
        ),
        in_specs=[vmem, hbm, hbm, vmem, hbm, hbm, hbm],
        out_specs=(hbm, hbm, vmem, hbm, hbm, hbm),
        scratch_shapes=[
            V(chunks, BF16),
            V(chunks, BF16),
            V(chunks, BF16),
            V(chunks, BF16),
            V(chunks, BF16),
            V((quarter, 2 * hidden), BF16),
            V((nk, hidden, kc), BF16),
            V((PASSES, 8, rows), F32),
            V((nd, PASSES, 8, rows), F32),
            V((PASSES, total, nd * rows), BF16),
            V((PASSES, nd * rows, total), BF16),
            V((2, nk, nd * rows, kc), BF16),
            V((nk, total, kc), BF16),
            V((4, nk, total, kc), BF16),
            V((total, 2 * hidden), F32),
            V((PASSES, total, 2 * hidden), BF16),
            V((total, hidden), BF16),
            V((PASSES, hidden, total), BF16),
            V((total, hidden), BF16),
            V((total, 2 * hidden), BF16),
            V((total, hidden), BF16),
            V((CAP, 2, half, 2 * hidden), BF16),
            V((CAP, 2, half, hidden), BF16),
            V((CAP, 2, 2, half, 2 * hidden), BF16),
            V((CAP, 2, 2, half, hidden), BF16),
            V((nk, total, kc), BF16),
            V((2, nk, total, kc), BF16),
            V((nk, nd * rows, kc), BF16),
            V((2,) + chunks, BF16),
            V((PASSES, rows, 1), F32),
            V((rows, kc), F32),
            V((nd, nk, 8, kc), F32),
            V((nd, nk, 8, kc), F32),
            V((ne, nk, 8, kc), F32),
            V((nd, nk, 8, kc), F32),
            S((4,)),
            S((4,)),
            S(()),
            S(()),
            S((4, nk)),
            S((4, nk)),
            S((4, nk, CAP)),
            S((4, nk, CAP)),
            S((4, nk, CAP)),
            S((4, nk, CAP)),
            S((4, nk)),
            S((4, nk)),
            S((2, nk)),
            S((2, nk)),
            S((4, CAP, 6)),
            S((4, CAP, 2)),
            S((4, CAP, 2, 2)),
            S((5, CAP, 6)),
            S((5, CAP, 3, 2)),
            S((3,)),
            S((3,)),
        ],
        compiler_params=pltpu.CompilerParams(
            collective_id=0, has_side_effects=True, vmem_limit_bytes=63_000_000
        ),
        cost_estimate=pl.CostEstimate(
            flops=36 * total * quarter * hidden, bytes_accessed=17 * 2**20, transcendentals=2 * total * hidden
        ),
    )(dest, tokens[0], cotangent[0], gain, w_gate[0, 0], w_up[0, 0], w_down[0, 0])
    out_rows, entry_grad, gain_total, grad_gate, grad_up, grad_down = pl.pallas_call(
        functools.partial(hand_over, quarter, kc),
        out_shape=(
            results[0],
            results[1],
            jax.ShapeDtypeStruct((1, width), F32),
            results[3],
            results[4],
            results[5],
        ),
        in_specs=[hbm, hbm, vmem, hbm, hbm, hbm],
        out_specs=(hbm, hbm, vmem, hbm, hbm, hbm),
        scratch_shapes=[V(results[i].shape, BF16) for i in (3, 4, 5, 0, 1)] + [S((2, 5, 2))],
        compiler_params=pltpu.CompilerParams(vmem_limit_bytes=40_000_000),
    )(*results)
    return (
        out_rows[None],
        entry_grad[None],
        gain_total,
        grad_gate[None, None],
        grad_up[None, None],
        grad_down[None, None],
    )


def solution(mesh):
    placed = (
        P("pipe", ("dp", "expert"), None),
        P("pipe", ("dp", "expert"), None),
        P("pipe", None),
        P("pipe", "expert", "dp", None),
        P("pipe", "expert", "dp", None),
        P("pipe", "expert", None, "dp"),
        P("pipe", None, ("dp", "expert"), None),
    )
    return jax.shard_map(
        body,
        mesh=mesh,
        in_specs=placed,
        out_specs=(
            P("pipe", ("dp", "expert"), None),
            P("pipe", ("dp", "expert"), None),
            P("pipe", None),
            P("pipe", "expert", "dp", None),
            P("pipe", "expert", "dp", None),
            P("pipe", "expert", None, "dp"),
        ),
        check_vma=False,
    )
```

```python
import functools
import math

import jax
import jax.numpy as jnp
from jax import lax
from jax.experimental import pallas as pl
from jax.experimental.pallas import tpu as pltpu
from jax.sharding import PartitionSpec as P

TILE = 8
CAP = 3
PASSES = 2
WIDTH = 256
epsilon = 1e-06
F32 = jnp.float32
BF16 = jnp.bfloat16


def kernel(
    sizes,
    dest, tok, cot, gain, wg, wu, wd,
    out_tok, grad_tok, gain_out, gg, gu, gd,
    tokc, cotc, hid1, grad0, norm, wgu, wdc, dest_own, dest_all, place, back,
    yin, xout, xin, acc, gate_up, act, act_t, grad_act,
    rs_f, rs_b, one_f, one_b, two_f, two_b,
    ret_out, ret_in, yret_out, yret_in, inverse, mean_acc, gain_acc, gain_dp, gain_ex, gain_all, way,
    load_sem, store_sem, dest_s, dest_r, y_s, y_r, x_s, x_r, rx_s, rx_r, ry_s, ry_r,
    z_s, z_r, way_s, way_r, sum_s, one_r, two_r, give_s, give_r, gain_s, gain_r,
):
    nd, npipe, ne, rows, width, hidden = sizes
    quarter = width // nd
    kc = min(WIDTH, quarter)
    nk = quarter // kc
    block = nd * CAP * TILE
    total = ne * block
    unit = nd * TILE
    lane = ne * unit
    lanes = range(CAP)
    half = lane // nd // 2
    q, p, e = lax.axis_index("dp"), lax.axis_index("pipe"), lax.axis_index("expert")
    q_up, q_down, q_far = lax.rem(q + 1, nd), lax.rem(q + nd - 1, nd), lax.rem(q + 2, nd)
    p_up, p_down = lax.rem(p + 1, npipe), lax.rem(p + npipe - 1, npipe)

    def send(src, dst, ssem, rsem, **where):
        pltpu.make_async_remote_copy(
            src_ref=src, dst_ref=dst, send_sem=ssem, recv_sem=rsem,
            device_id=where, device_id_type=pl.DeviceIdType.MESH,
        ).start()

    def drain(ref, sem):
        pltpu.make_async_copy(ref, ref, sem).wait()

    def loop(count, step):
        lax.fori_loop(0, count, lambda i, c: (step(i), c)[1], 0)

    def at(i, size):
        return pl.ds(pl.multiple_of(i * size, size), size)

    def rows_of(g, i):
        return pl.ds(pl.multiple_of(g * lane + i * unit, unit), unit)

    def span_of(g):
        return slice(g * lane, (g + 1) * lane)

    def gain_of(k, j):
        return gain[0:1, pl.ds(pl.multiple_of(j * quarter + k * kc, kc), kc)]

    for k in range(nk):
        for j in range(nd):
            cols = pl.ds(j * quarter + k * kc, kc)
            pltpu.make_async_copy(tok.at[:, cols], tokc.at[k, j], load_sem.at[0]).start()
    pltpu.make_async_copy(wg, wgu.at[:, 0:hidden], load_sem.at[1]).start()
    pltpu.make_async_copy(wu, wgu.at[:, hidden : 2 * hidden], load_sem.at[1]).start()
    for k in range(nk):
        pltpu.make_async_copy(wd.at[:, pl.ds(k * kc, kc)], wdc.at[k], load_sem.at[2]).start()
    for k in range(nk):
        for j in range(nd):
            cols = pl.ds(j * quarter + k * kc, kc)
            pltpu.make_async_copy(cot.at[:, cols], cotc.at[k, j], load_sem.at[3]).start()

    barrier = pltpu.get_barrier_semaphore()

    def greet(**where):
        pl.semaphore_signal(barrier, inc=1, device_id=where, device_id_type=pl.DeviceIdType.MESH)

    for d in range(1, nd):
        greet(dp=lax.rem(q + d, nd))
    for d in range(1, ne):
        greet(expert=lax.rem(e + d, ne))
    greet(pipe=p_up)
    greet(pipe=p_down)

    drain(tokc, load_sem.at[0])

    def squares(ref, k, before):
        for j in range(nd):
            wide = ref[k, j].astype(F32)
            before = before + wide * wide
        return before

    def scale(t, squared):
        inverse[t] = lax.rsqrt(jnp.sum(squared, axis=-1, keepdims=True) / width + epsilon)

    def normalize(t, ref, k):
        for j in range(nd):
            norm[k, j] = (ref[k, j].astype(F32) * inverse[t] * gain_of(k, j)).astype(BF16)

    none = jnp.zeros((rows, kc), F32)
    scale(0, lax.fori_loop(0, nk, lambda k, c: squares(tokc, k, c), none))
    pl.semaphore_wait(barrier, nd - 1 + ne - 1 + 2)

    def work_out_places():
        row_tile = lax.broadcasted_iota(jnp.int32, (rows, rows), 1) // TILE
        row_at = lax.broadcasted_iota(jnp.int32, (1, rows), 1)
        earlier = (row_tile.T < row_tile)
        for t in range(PASSES):
            expert_of = jnp.broadcast_to(dest[t, 0:1, :], (rows, rows))
            same = jnp.where(earlier & (expert_of.T == expert_of), 1.0, 0.0).astype(F32)
            rank = jnp.sum(same, axis=0, keepdims=True) / TILE
            inner = (q * TILE + row_at % TILE).astype(F32)
            mine = dest[t, 0:1, :]
            dest_own[t] = jnp.broadcast_to(rank * lane + mine * unit + inner, (8, rows))
        for d in range(1, nd):
            send(dest_own, dest_all.at[q], dest_s, dest_r, dp=lax.rem(q + d, nd))
        dest_all[q] = dest_own[...]

    def build_places():
        drain(dest_all.at[0 : nd - 1], dest_r)
        slot_ids = lax.broadcasted_iota(jnp.int32, (total, rows), 0).astype(F32)
        for t in range(PASSES):
            for s in range(nd):
                hot = jnp.where(slot_ids == dest_all[s, t, 0:1, :], 1.0, 0.0).astype(F32)
                place[t, :, s * rows : (s + 1) * rows] = hot.astype(BF16)
                back[t, s * rows : (s + 1) * rows, :] = hot.T.astype(BF16)


    def y_send(ph, st, src, k):
        for d in range(1, nd):
            j = lax.rem(q + d, nd)
            send(src.at[k, j], yin.at[st, k, at(q, rows)], y_s.at[ph, k], y_r.at[ph, k], dp=j)
        yin[st, k, at(q, rows), :] = src[k, q]

    def y_wait(ph, st, k):
        drain(yin.at[st, k, 0 : (nd - 1) * rows], y_r.at[ph, k])

    def x_send(ph, st, t, k, g):
        mine = span_of(g)
        xout[k, mine, :] = jnp.dot(place[t, mine, :], yin[st, k], preferred_element_type=F32).astype(BF16)
        for d in range(1, ne):
            o = lax.rem(e + d, ne)
            send(xout.at[k, rows_of(g, o)], xin.at[ph, k, rows_of(g, e)], x_s.at[ph, k, g], x_r.at[ph, k, g], expert=o)
        xin[ph, k, rows_of(g, e), :] = xout[k, rows_of(g, e), :]

    def x_wait(ph, k, g):
        drain(xin.at[ph, k, 0 : (ne - 1) * unit], x_r.at[ph, k, g])

    def forward_chunk(ph, k, g):
        x_wait(ph, k, g)
        mine = span_of(g)
        acc[mine, :] += jnp.dot(xin[ph, k, mine, :], wgu[at(k, kc), :], preferred_element_type=F32)

    def backward_chunk(ph, k):
        for g in lanes:
            x_wait(ph, k, g)

        def some(m):
            there = at(m, lane)
            acc[there, 0:hidden] += lax.dot_general(
                xin[ph, k, there, :], wdc[k], (((1,), (1,)), ((), ())), preferred_element_type=F32
            )

        loop(CAP, some)

    def settle_y(ph, st):
        loop(nk, lambda k: drain(yin.at[st, k, 0 : (nd - 1) * rows], y_s.at[ph, k]))

    def settle_x(ph):
        def step(k):
            for g in lanes:
                drain(xout.at[k, 0 : (ne - 1) * unit], x_s.at[ph, k, g])

        loop(nk, step)

    def span(g, b, h):
        return pl.ds(pl.multiple_of(g * lane + (2 * b + h) * half, half), half)

    def summing(ph, src, one, two):
        def open_(g):
            send(src.at[span(g, q_far, 0)], one.at[g, 0], sum_s.at[ph, g, 0], one_r.at[ph, g, 0], dp=q_down)
            send(src.at[span(g, q_far, 1)], one.at[g, 1], sum_s.at[ph, g, 1], one_r.at[ph, g, 1], dp=q_up)
            send(src.at[span(g, q_down, 1)], two.at[g, 0, 1], sum_s.at[ph, g, 2], two_r.at[ph, g, 0, 1], dp=q_down)
            send(src.at[span(g, q_up, 0)], two.at[g, 1, 0], sum_s.at[ph, g, 3], two_r.at[ph, g, 1, 0], dp=q_up)

        def middle(g):
            for side, b in ((0, q_down), (1, q_up)):
                drain(one.at[g, side], one_r.at[ph, g, side])
                there = span(g, b, side)
                src[there, :] = (src[there, :].astype(F32) + one[g, side].astype(F32)).astype(BF16)
                send(src.at[there], two.at[g, side, side], sum_s.at[ph, g, 4 + side], two_r.at[ph, g, side, side], dp=b)

        def whole(g, h):
            for side in range(2):
                drain(two.at[g, side, h], two_r.at[ph, g, side, h])
            return src[span(g, q, h), :].astype(F32) + two[g, 0, h].astype(F32) + two[g, 1, h].astype(F32)

        def settle(g):
            for i in range(6):
                drain(src.at[0:half], sum_s.at[ph, g, i])

        return open_, middle, whole, settle

    def giving(ph, dst):
        def offer(g):
            for i in range(2):
                up, down = span(g, q, i), span(g, q, 1 - i)
                send(dst.at[up], dst.at[up], give_s.at[ph, g, i], give_r.at[ph, g, 0, i], dp=q_up)
                send(dst.at[down], dst.at[down], give_s.at[ph, g, 2 + i], give_r.at[ph, g, 1, 1 - i], dp=q_down)

        def pass_on(g):
            first, second = span(g, q_down, 0), span(g, q_up, 1)
            drain(dst.at[first], give_r.at[ph, g, 0, 0])
            send(dst.at[first], dst.at[first], give_s.at[ph, g, 4], give_r.at[ph, g, 2, 0], dp=q_up)
            drain(dst.at[second], give_r.at[ph, g, 1, 1])
            send(dst.at[second], dst.at[second], give_s.at[ph, g, 5], give_r.at[ph, g, 2, 1], dp=q_down)

        def close(g):
            drain(dst.at[span(g, q_down, 1)], give_r.at[ph, g, 0, 1])
            drain(dst.at[span(g, q_up, 0)], give_r.at[ph, g, 1, 0])
            drain(dst.at[span(g, q_far, 0)], give_r.at[ph, g, 2, 0])
            drain(dst.at[span(g, q_far, 1)], give_r.at[ph, g, 2, 1])

        def settle(g):
            for i in range(6):
                drain(dst.at[0:half], give_s.at[ph, g, i])

        return offer, pass_on, close, settle

    def small_steps(g, step):
        size = math.gcd(64, lane)
        lax.fori_loop(g * (lane // size), (g + 1) * (lane // size), lambda m, c: (step(at(m, size)), c)[1], 0)

    def round_into(src, columns, g):
        def some(there):
            src[there, :] = acc[there, 0:columns].astype(BF16)

        small_steps(g, some)

    def ret_send(ph, st, g, k):
        for d in range(1, ne):
            o = lax.rem(e + d, ne)
            send(
                ret_out.at[k, rows_of(g, o)], ret_in.at[st, k, rows_of(g, e)],
                rx_s.at[ph, k, g], rx_r.at[ph, k, g], expert=o,
            )
        ret_in[st, k, rows_of(g, e), :] = ret_out[k, rows_of(g, e), :]

    def settle_ret(ph, g):
        loop(nk, lambda k: drain(ret_out.at[k, 0 : (ne - 1) * unit], rx_s.at[ph, k, g]))

    def settle_yret(ph):
        loop(nk, lambda k: drain(yret_out.at[k, 0 : (nd - 1) * rows], ry_s.at[ph, k]))

    short = nd * rows // 2

    def collect_late(ph, st, t, k):
        for g in lanes:
            drain(ret_in.at[st, k, 0 : (ne - 1) * unit], rx_r.at[ph, k, g])
        for j in range(nd):
            norm[k, j] = jnp.dot(
                back[t, j * rows : (j + 1) * rows, :], ret_in[st, k], preferred_element_type=F32
            ).astype(BF16)
        for d in range(1, nd):
            j = lax.rem(q + d, nd)
            send(norm.at[k, j], yret_in.at[st, k, q], ry_s.at[ph, k], ry_r.at[ph, k], dp=j)
        yret_in[st, k, q] = norm[k, q]

    def collect(ph, st, t, k):
        for g in lanes:
            drain(ret_in.at[st, k, 0 : (ne - 1) * unit], rx_r.at[ph, k, g])

        def some(m):
            yret_out[k, at(m, short), :] = jnp.dot(
                back[t, at(m, short), :], ret_in[st, k], preferred_element_type=F32
            ).astype(BF16)

        loop(2, some)
        for d in range(1, nd):
            j = lax.rem(q + d, nd)
            send(yret_out.at[k, at(j, rows)], yret_in.at[st, k, q], ry_s.at[ph, k], ry_r.at[ph, k], dp=j)
        yret_in[st, k, q] = yret_out[k, at(q, rows), :]

    def landed(ph, st, k):
        drain(yret_in.at[st, k, 0 : nd - 1], ry_r.at[ph, k])

    def activate(t, g):
        def some(there):
            gate = gate_up[t, there, 0:hidden].astype(F32)
            up = gate_up[t, there, hidden : 2 * hidden].astype(F32)
            act[there, :] = (gate * jax.nn.sigmoid(gate) * up).astype(BF16)

        small_steps(g, some)

    def forward_down(ph, g, beside=None):
        mine = span_of(g)

        def down(k):
            ret_out[k, mine, :] = jnp.dot(act[mine, :], wdc[k], preferred_element_type=F32).astype(BF16)
            ret_send(ph, 0, g, k)
            if beside is not None:
                beside(k)

        loop(nk, down)

    def turn(t):
        wide = math.gcd(total, 128)
        for m in range(total // wide):
            act_t[t, :, m * wide : (m + 1) * wide] = act[m * wide : (m + 1) * wide, :].T

    def pre_grads(gate, up, grad):
        s = jax.nn.sigmoid(gate)
        silu = gate * s
        return grad * up * s * (1.0 + gate * (1.0 - s)), grad * silu, silu * up

    def before(t, g):
        def some(there):
            gate = gate_up[t, there, 0:hidden].astype(F32)
            up = gate_up[t, there, hidden : 2 * hidden].astype(F32)
            of_gate, of_up, _ = pre_grads(gate, up, grad_act[there, :].astype(F32))
            gate_up[t, there, 0:hidden] = of_gate.astype(BF16)
            gate_up[t, there, hidden : 2 * hidden] = of_up.astype(BF16)

        small_steps(g, some)

    def backward_up(ph, t, g):
        mine = span_of(g)

        def up_(k):
            ret_out[k, mine, :] = lax.dot_general(
                gate_up[t, mine, :], wgu[at(k, kc), :], (((1,), (1,)), ((), ())), preferred_element_type=F32
            ).astype(BF16)
            ret_send(ph, 1, g, k)

        loop(nk, up_)

    def to_rows(ref, k, out, sem):
        for j in range(nd):
            cols = pl.ds(pl.multiple_of(j * quarter + k * kc, kc), kc)
            pltpu.make_async_copy(ref.at[k, j], out.at[:, cols], sem).start()

    def add_rows(ph, ref, k):
        landed(ph, 0, k)
        for j in range(nd):
            yret_in[0, k, j] = (ref[k, j].astype(F32) + yret_in[0, k, j].astype(F32)).astype(BF16)

    def terms(t, ref, k, j):
        return yret_in[1, k, j].astype(F32), ref[k, j].astype(F32) * inverse[t]

    def gather_grads(ph, t, ref, k):
        landed(ph, 1, k)
        fresh = mean_acc[...]
        for j in range(nd):
            u, scaled = terms(t, ref, k, j)
            both = u * scaled
            gain_acc[j, k] += jnp.sum(both.reshape(rows // 8, 8, kc), axis=0)
            fresh = fresh + both * gain_of(k, j)
        mean_acc[...] = fresh

    def finish_grads(t, ref, grad_ref, k, mean):
        for j in range(nd):
            u, scaled = terms(t, ref, k, j)
            wide = inverse[t] * (u * gain_of(k, j) - scaled * mean)
            yret_in[1, k, j] = (grad_ref[k, j].astype(F32) + wide).astype(BF16)

    def mean_of():
        return jnp.sum(mean_acc[...], axis=-1, keepdims=True) / width

    def weight_grads(k):
        both = jnp.zeros((kc, 2 * hidden), F32)
        for t in range(PASSES):
            both = both + lax.dot_general(
                xin[t, k], gate_up[t], (((0,), (0,)), ((), ())), preferred_element_type=F32
            )
        wgu[at(k, kc), :] = both.astype(BF16)
        pltpu.make_async_copy(wgu.at[at(k, kc), 0:hidden], gg.at[at(k, kc)], store_sem.at[2]).start()
        pltpu.make_async_copy(wgu.at[at(k, kc), hidden : 2 * hidden], gu.at[at(k, kc)], store_sem.at[2]).start()
        down = jnp.zeros((hidden, kc), F32)
        for t, ph in ((0, 3), (1, 2)):
            down = down + jnp.dot(act_t[t], xin[ph, k], preferred_element_type=F32)
        wdc[k] = down.astype(BF16)
        pltpu.make_async_copy(wdc.at[k], gd.at[:, at(k, kc)], store_sem.at[3]).start()

    def long_way(d, src, dst, where):
        def leave_():
            send(src, way.at[d, 0], z_s.at[d, 0], way_r.at[d, 0], pipe=where)

        def hop1():
            drain(way.at[d, 0], way_r.at[d, 0])
            send(way.at[d, 0], way.at[d, 1], way_s.at[d, 0], way_r.at[d, 1], pipe=where)

        def hop2():
            drain(way.at[d, 1], way_r.at[d, 1])
            send(way.at[d, 1], dst, way_s.at[d, 1], z_r.at[d, 0], pipe=where)

        return leave_, hop1, hop2

    def when(test, step):
        @pl.when(test)
        def _():
            step()

    lag = 2

    def forward_to_sums(ph, st, t, sums, mine, gives):
        open_, middle = sums[0], sums[1]
        acc[...] = jnp.zeros_like(acc)

        def step(i):
            for g in lanes:
                def first(g=g):
                    if g == 0:
                        y_wait(ph, st, i)
                    x_send(ph, st, t, i - g * lag, g)

                when((i >= g * lag) & (i < nk + g * lag), first)
            for g in lanes:
                when((i >= g * lag + 1) & (i < nk + g * lag + 1), lambda g=g: forward_chunk(ph, i - g * lag - 1, g))

        def start(g):
            round_into(rs_f, 2 * hidden, g)
            open_(g)

        def run(first, last):
            lax.fori_loop(first, last, lambda i, c: (step(i), c)[1], 0)

        run(0, nk + 1)
        start(0)
        run(nk + 1, nk + 2)
        middle(0)
        run(nk + 2, nk + 3)
        start(1)
        mine(0)
        run(nk + 3, nk + 4)
        gives[1](0)
        middle(1)
        run(nk + 4, nk + 5)
        start(2)
        mine(1)
        middle(2)

    def norm_out0(k):
        normalize(0, tokc, k)
        y_send(0, 0, norm, k)

    loop(nk, norm_out0)
    work_out_places()
    gain_acc[...] = jnp.zeros_like(gain_acc)
    build_places()
    drain(wgu, load_sem.at[1])
    drain(wdc, load_sem.at[2])
    drain(cotc, load_sem.at[3])

    sums = summing(0, rs_f, one_f, two_f)
    gives = giving(0, gate_up.at[0])

    def mine0(g):
        for h in range(2):
            gate_up[0, span(g, q, h), :] = sums[2](g, h).astype(BF16)
        gives[0](g)

    forward_to_sums(0, 0, 0, sums, mine0, gives)
    gives[2](0)
    activate(0, 0)
    forward_down(0, 0)
    gives[1](1)
    mine0(2)
    settle_y(0, 0)
    settle_x(0)
    gives[2](1)
    activate(0, 1)
    forward_down(0, 1)
    gives[1](2)
    acc[:, 0:hidden] = jnp.zeros((total, hidden), F32)
    gives[2](2)
    activate(0, 2)
    forward_down(0, 2, lambda k: y_send(2, 1, cotc, k))

    round0 = long_way(0, yret_in.at[0, 0], hid1.at[0], p_down)

    def turn_round(i):
        def second():
            k = i - 1
            add_rows(0, tokc, k)
            when(k == 0, round0[0])
            when(
                k > 0,
                lambda: send(yret_in.at[0, k], hid1.at[k], z_s.at[0, k], z_r.at[0, k], pipe=p_up),
            )
            y_wait(2, 1, k)
            for g in lanes:
                x_send(2, 1, 1, k, g)

        when(i < nk, lambda: collect(0, 0, 0, i))
        when((i >= 1) & (i <= nk), second)
        when(i >= 2, lambda: backward_chunk(2, i - 2))
        when(i == hop_at[0], round0[1])
        when(i == hop_at[1], round0[2])

    hop_at = (min(3, nk), min(5, nk + 1))
    loop(nk + 2, turn_round)
    sums_b = summing(2, rs_b, one_b, two_b)
    for g in lanes:
        round_into(rs_b, hidden, g)
        sums_b[0](g)
    turn(0)
    for g in lanes:
        sums[3](g)
        gives[3](g)
        settle_ret(0, g)
    settle_yret(0)
    settle_y(2, 1)
    settle_x(2)

    def arrived(k, c):
        drain(hid1.at[k], z_r.at[0, k])
        return squares(hid1, k, c)

    so_far = lax.fori_loop(1, nk, arrived, none)
    for g in lanes:
        sums_b[1](g)
    scale(1, arrived(0, so_far))
    loop(nk, lambda k: drain(yret_in.at[0, k], z_s.at[0, k]))

    def norm_out1(k):
        normalize(1, hid1, k)
        y_send(1, 0, norm, k)

    loop(nk, norm_out1)
    sums = summing(1, rs_f, one_f, two_f)
    gives = giving(1, gate_up.at[1])

    def mine1(g):
        for h in range(2):
            there = span(g, q, h)
            both = sums[2](g, h)
            of_gate, of_up, activated = pre_grads(both[:, 0:hidden], both[:, hidden : 2 * hidden], sums_b[2](g, h))
            gate_up[1, there, 0:hidden] = of_gate.astype(BF16)
            gate_up[1, there, hidden : 2 * hidden] = of_up.astype(BF16)
            act[there, :] = activated.astype(BF16)
        gives[0](g)

    forward_to_sums(1, 0, 1, sums, mine1, gives)

    gives[2](0)
    backward_up(2, 1, 0)
    gives[1](1)
    mine1(2)
    settle_y(1, 0)
    settle_x(1)
    gives[2](1)
    backward_up(2, 1, 1)
    gives[1](2)
    mean_acc[...] = jnp.zeros_like(mean_acc)
    gives[2](2)
    backward_up(2, 1, 2)

    def back1(i):
        when(i < nk, lambda: collect(2, 1, 1, i))
        when(i >= 1, lambda: gather_grads(2, 1, hid1, i - 1))

    loop(nk + 1, back1)
    mean = mean_of()

    round1 = long_way(1, yret_in.at[1, 0], grad0.at[0], p_up)

    def leave(k):
        finish_grads(1, hid1, cotc, k, mean)
        when(k == 0, round1[0])
        when(
            k > 0,
            lambda: send(yret_in.at[1, k], grad0.at[k], z_s.at[1, k], z_r.at[1, k], pipe=p_down),
        )

    loop(nk, leave)

    acts = giving(4, act)
    for g in lanes:
        acts[0](g)
    for g in lanes:
        sums[3](g)
        gives[3](g)
        sums_b[3](g)
        settle_ret(2, g)
    settle_yret(2)
    acc[:, 0:hidden] = jnp.zeros((total, hidden), F32)

    def come(i):
        def first():
            k = lax.rem(i + 1, nk)
            drain(grad0.at[k], z_r.at[1, k])
            y_send(3, 1, grad0, k)

        def second():
            k = lax.rem(i, nk)
            y_wait(3, 1, k)
            for g in lanes:
                x_send(3, 1, 0, k, g)

        when(i < nk, first)
        when((i >= 1) & (i <= nk), second)
        when(i >= 2, lambda: backward_chunk(3, lax.rem(i - 1, nk)))
        when(i == 1, round1[2])

    loop(1, come)
    round1[1]()
    for g in lanes:
        acts[1](g)
    for g in lanes:
        acts[2](g)
    forward_down(1, 0)
    turn(1)
    lax.fori_loop(1, nk + 2, lambda i, c: (come(i), c)[1], 0)
    loop(nk, lambda k: drain(yret_in.at[1, k], z_s.at[1, k]))
    sums_b = summing(3, rs_b, one_b, two_b)
    gives = giving(3, grad_act)

    def mine3(g):
        for h in range(2):
            grad_act[span(g, q, h), :] = sums_b[2](g, h).astype(BF16)
        gives[0](g)

    for g in lanes:
        round_into(rs_b, hidden, g)
        sums_b[0](g)
    forward_down(1, 1)
    for g in lanes:
        sums_b[1](g)
    forward_down(1, 2)
    for g in lanes:
        mine3(g)
        if g >= 1:
            gives[1](g - 1)
    gives[1](CAP - 1)
    settle_y(3, 1)
    settle_x(3)
    for g in lanes:
        gives[2](g)
        before(0, g)
        settle_ret(1, g)
        backward_up(3, 0, g)

    early = min(2, nk)
    loop(early, lambda k: collect_late(1, 0, 1, k))
    mean_acc[...] = jnp.zeros_like(mean_acc)

    def back0(i):
        when(i < nk, lambda: collect(3, 1, 0, i))
        when(i >= 1, lambda: gather_grads(3, 0, tokc, i - 1))
        when(i < nk - 1, lambda: weight_grads(i))

    loop(nk + 1, back0)
    for d in range(1, nd):
        j = lax.rem(q + d, nd)
        send(gain_acc.at[j], gain_dp.at[q], gain_s.at[0], gain_r.at[0], dp=j)
    lax.fori_loop(early, nk, lambda k, c: (collect_late(1, 0, 1, k), c)[1], 0)
    mean = mean_of()

    def last(k):
        finish_grads(0, tokc, grad0, k, mean)
        to_rows(yret_in.at[1], k, grad_tok, store_sem.at[1])

    loop(nk, last)

    gain_dp[q] = gain_acc[q]
    drain(gain_dp.at[0 : nd - 1], gain_r.at[0])
    mine = gain_dp[0]
    for j in range(1, nd):
        mine = mine + gain_dp[j]
    gain_ex[e] = mine
    for d in range(1, ne):
        send(gain_ex.at[e], gain_ex.at[e], gain_s.at[1], gain_r.at[1], expert=lax.rem(e + d, ne))
    weight_grads(nk - 1)

    def leave1(k):
        add_rows(1, hid1, k)
        to_rows(yret_in.at[0], k, out_tok, store_sem.at[0])

    loop(nk, leave1)
    drain(gain_ex.at[0 : ne - 1], gain_r.at[1])
    mine = gain_ex[0]
    for j in range(1, ne):
        mine = mine + gain_ex[j]
    gain_all[q] = mine
    for d in range(1, nd):
        send(gain_all.at[q], gain_all.at[q], gain_s.at[2], gain_r.at[2], dp=lax.rem(q + d, nd))
    drain(gain_all.at[0 : nd - 1], gain_r.at[2])
    gain_out[...] = jnp.broadcast_to(jnp.sum(gain_all[...], axis=2, keepdims=True), gain_out.shape)

    for g in lanes:
        sums_b[3](g)
        gives[3](g)
        acts[3](g)
        settle_ret(3, g)
    settle_yret(3)
    loop(nk, lambda k: drain(norm.at[k, 0 : nd - 1], ry_s.at[1, k]))
    for d in range(2):
        for i in range(2):
            drain(way.at[d, i], way_s.at[d, i])
    drain(gain_dp.at[0 : nd - 1], gain_s.at[0])
    drain(gain_ex.at[0 : ne - 1], gain_s.at[1])
    drain(gain_all.at[0 : nd - 1], gain_s.at[2])
    drain(dest_all.at[0 : nd - 1], dest_s)
    drain(yret_in.at[0], store_sem.at[0])
    drain(yret_in.at[1], store_sem.at[1])
    drain(wgu, store_sem.at[2])
    drain(wdc, store_sem.at[3])


def hand_over(quarter, kc, *refs):
    got, given, stages, sems = refs[0:6], refs[6:12], refs[12:17], refs[17]
    order = (3, 4, 5, 0, 1)

    def piece(n, h, way):
        size = stages[n].shape[0] // 2
        part = pl.ds(h * size, size)
        ends = (got[order[n]].at[part], stages[n].at[part], given[order[n]].at[part])
        return pltpu.make_async_copy(ends[way], ends[way + 1], sems.at[way, n, h])

    each = [(n, h) for n in range(len(order)) for h in range(2)]
    for n, h in each:
        piece(n, h, 0).start()
    for j in range(got[2].shape[0]):
        for k in range(got[2].shape[1]):
            given[2][0:1, j * quarter + k * kc : j * quarter + (k + 1) * kc] = got[2][j, k, 0:1, :]
    for n, h in each:
        piece(n, h, 0).wait()
        piece(n, h, 1).start()
    for n, h in each:
        piece(n, h, 1).wait()


def body(tokens, cotangent, gain, w_gate, w_up, w_down, route):
    npipe, nd, ne = lax.axis_size("pipe"), lax.axis_size("dp"), lax.axis_size("expert")
    section = lax.axis_index("pipe")
    rows, width = tokens.shape[1:]
    quarter, hidden = w_gate.shape[2:]
    kc = min(WIDTH, quarter)
    nk = quarter // kc
    block = nd * CAP * TILE
    total = ne * block
    half = total // CAP // nd // 2
    table = route[0, :, :, 0]
    dest = []
    for t in range(PASSES):
        micro = (section - t + npipe) % npipe
        now = lax.dynamic_index_in_dim(table, micro, 0, keepdims=False)
        dest.append(now.astype(F32))
    dest = jnp.broadcast_to(jnp.stack(dest)[:, None, :, None], (PASSES, 8, rows // TILE, TILE))
    dest = dest.reshape(PASSES, 8, rows)

    hbm = pl.BlockSpec(memory_space=pl.ANY)
    vmem = pl.BlockSpec(memory_space=pltpu.VMEM)
    V = pltpu.VMEM
    S = pltpu.SemaphoreType.DMA
    chunks = (nk, nd, rows, kc)
    results = pl.pallas_call(
        functools.partial(kernel, (nd, npipe, ne, rows, width, hidden)),
        out_shape=(
            jax.ShapeDtypeStruct((rows, width), BF16),
            jax.ShapeDtypeStruct((rows, width), BF16),
            jax.ShapeDtypeStruct((nd, nk, 8, kc), F32),
            jax.ShapeDtypeStruct((quarter, hidden), BF16),
            jax.ShapeDtypeStruct((quarter, hidden), BF16),
            jax.ShapeDtypeStruct((hidden, quarter), BF16),
        ),
        in_specs=[vmem, hbm, hbm, vmem, hbm, hbm, hbm],
        out_specs=(hbm, hbm, vmem, hbm, hbm, hbm),
        scratch_shapes=[
            V(chunks, BF16),
            V(chunks, BF16),
            V(chunks, BF16),
            V(chunks, BF16),
            V(chunks, BF16),
            V((quarter, 2 * hidden), BF16),
            V((nk, hidden, kc), BF16),
            V((PASSES, 8, rows), F32),
            V((nd, PASSES, 8, rows), F32),
            V((PASSES, total, nd * rows), BF16),
            V((PASSES, nd * rows, total), BF16),
            V((2, nk, nd * rows, kc), BF16),
            V((nk, total, kc), BF16),
            V((4, nk, total, kc), BF16),
            V((total, 2 * hidden), F32),
            V((PASSES, total, 2 * hidden), BF16),
            V((total, hidden), BF16),
            V((PASSES, hidden, total), BF16),
            V((total, hidden), BF16),
            V((total, 2 * hidden), BF16),
            V((total, hidden), BF16),
            V((CAP, 2, half, 2 * hidden), BF16),
            V((CAP, 2, half, hidden), BF16),
            V((CAP, 2, 2, half, 2 * hidden), BF16),
            V((CAP, 2, 2, half, hidden), BF16),
            V((nk, total, kc), BF16),
            V((2, nk, total, kc), BF16),
            V((nk, nd * rows, kc), BF16),
            V((2,) + chunks, BF16),
            V((PASSES, rows, 1), F32),
            V((rows, kc), F32),
            V((nd, nk, 8, kc), F32),
            V((nd, nk, 8, kc), F32),
            V((ne, nk, 8, kc), F32),
            V((nd, nk, 8, kc), F32),
            V((2, 2) + chunks[1:], BF16),
            S((4,)),
            S((4,)),
            S(()),
            S(()),
            S((4, nk)),
            S((4, nk)),
            S((4, nk, CAP)),
            S((4, nk, CAP)),
            S((4, nk, CAP)),
            S((4, nk, CAP)),
            S((4, nk)),
            S((4, nk)),
            S((2, nk)),
            S((2, nk)),
            S((2, 2)),
            S((2, 2)),
            S((4, CAP, 6)),
            S((4, CAP, 2)),
            S((4, CAP, 2, 2)),
            S((5, CAP, 6)),
            S((5, CAP, 3, 2)),
            S((3,)),
            S((3,)),
        ],
        compiler_params=pltpu.CompilerParams(
            collective_id=0, has_side_effects=True, vmem_limit_bytes=63_000_000
        ),
        cost_estimate=pl.CostEstimate(
            flops=36 * total * quarter * hidden, bytes_accessed=17 * 2**20, transcendentals=2 * total * hidden
        ),
    )(dest, tokens[0], cotangent[0], gain, w_gate[0, 0], w_up[0, 0], w_down[0, 0])
    out_rows, entry_grad, gain_total, grad_gate, grad_up, grad_down = pl.pallas_call(
        functools.partial(hand_over, quarter, kc),
        out_shape=(
            results[0],
            results[1],
            jax.ShapeDtypeStruct((1, width), F32),
            results[3],
            results[4],
            results[5],
        ),
        in_specs=[hbm, hbm, vmem, hbm, hbm, hbm],
        out_specs=(hbm, hbm, vmem, hbm, hbm, hbm),
        scratch_shapes=[V(results[i].shape, BF16) for i in (3, 4, 5, 0, 1)] + [S((2, 5, 2))],
        compiler_params=pltpu.CompilerParams(vmem_limit_bytes=40_000_000),
    )(*results)
    return (
        out_rows[None],
        entry_grad[None],
        gain_total,
        grad_gate[None, None],
        grad_up[None, None],
        grad_down[None, None],
    )


def solution(mesh):
    placed = (
        P("pipe", ("dp", "expert"), None),
        P("pipe", ("dp", "expert"), None),
        P("pipe", None),
        P("pipe", "expert", "dp", None),
        P("pipe", "expert", "dp", None),
        P("pipe", "expert", None, "dp"),
        P("pipe", None, ("dp", "expert"), None),
    )
    return jax.shard_map(
        body,
        mesh=mesh,
        in_specs=placed,
        out_specs=(
            P("pipe", ("dp", "expert"), None),
            P("pipe", ("dp", "expert"), None),
            P("pipe", None),
            P("pipe", "expert", "dp", None),
            P("pipe", "expert", "dp", None),
            P("pipe", "expert", None, "dp"),
        ),
        check_vma=False,
    )
```

```python
import functools
import math

import jax
import jax.numpy as jnp
from jax import lax
from jax.experimental import pallas as pl
from jax.experimental.pallas import tpu as pltpu
from jax.sharding import PartitionSpec as P

TILE = 8
CAP = 3
PASSES = 2
WIDTH = 256
epsilon = 1e-06
F32 = jnp.float32
BF16 = jnp.bfloat16


def kernel(
    sizes,
    dest, tok, cot, gain, wg, wu, wd,
    out_tok, grad_tok, gain_out, gg, gu, gd,
    tokc, cotc, hid1, grad0, norm, wgu, wdc, dest_own, dest_all, place, back,
    yin, xout, xin, acc, gate_up, act, act_t, grad_act,
    rs_f, rs_b, one_f, one_b, two_f, two_b,
    ret_out, ret_in, yret_out, yret_in, inverse, mean_acc, gain_acc, gain_dp, gain_ex, gain_all, way,
    load_sem, store_sem, dest_s, dest_r, y_s, y_r, x_s, x_r, rx_s, rx_r, ry_s, ry_r,
    z_s, z_r, way_s, way_r, sum_s, one_r, two_r, give_s, give_r, gain_s, gain_r,
):
    nd, npipe, ne, rows, width, hidden = sizes
    quarter = width // nd
    kc = min(WIDTH, quarter)
    nk = quarter // kc
    block = nd * CAP * TILE
    total = ne * block
    unit = nd * TILE
    lane = ne * unit
    lanes = range(CAP)
    half = lane // nd // 2
    q, p, e = lax.axis_index("dp"), lax.axis_index("pipe"), lax.axis_index("expert")
    q_up, q_down, q_far = lax.rem(q + 1, nd), lax.rem(q + nd - 1, nd), lax.rem(q + 2, nd)
    p_up, p_down = lax.rem(p + 1, npipe), lax.rem(p + npipe - 1, npipe)

    def send(src, dst, ssem, rsem, **where):
        pltpu.make_async_remote_copy(
            src_ref=src, dst_ref=dst, send_sem=ssem, recv_sem=rsem,
            device_id=where, device_id_type=pl.DeviceIdType.MESH,
        ).start()

    def drain(ref, sem):
        pltpu.make_async_copy(ref, ref, sem).wait()

    def loop(count, step):
        lax.fori_loop(0, count, lambda i, c: (step(i), c)[1], 0)

    def at(i, size):
        return pl.ds(pl.multiple_of(i * size, size), size)

    def rows_of(g, i):
        return pl.ds(pl.multiple_of(g * lane + i * unit, unit), unit)

    def span_of(g):
        return slice(g * lane, (g + 1) * lane)

    def gain_of(k, j):
        return gain[0:1, pl.ds(pl.multiple_of(j * quarter + k * kc, kc), kc)]

    for k in range(nk):
        for j in range(nd):
            cols = pl.ds(j * quarter + k * kc, kc)
            pltpu.make_async_copy(tok.at[:, cols], tokc.at[k, j], load_sem.at[0]).start()
    pltpu.make_async_copy(wg, wgu.at[:, 0:hidden], load_sem.at[1]).start()
    pltpu.make_async_copy(wu, wgu.at[:, hidden : 2 * hidden], load_sem.at[1]).start()
    for k in range(nk):
        pltpu.make_async_copy(wd.at[:, pl.ds(k * kc, kc)], wdc.at[k], load_sem.at[2]).start()
    for k in range(nk):
        for j in range(nd):
            cols = pl.ds(j * quarter + k * kc, kc)
            pltpu.make_async_copy(cot.at[:, cols], cotc.at[k, j], load_sem.at[3]).start()

    barrier = pltpu.get_barrier_semaphore()

    def greet(**where):
        pl.semaphore_signal(barrier, inc=1, device_id=where, device_id_type=pl.DeviceIdType.MESH)

    for d in range(1, nd):
        greet(dp=lax.rem(q + d, nd))
    for d in range(1, ne):
        greet(expert=lax.rem(e + d, ne))
    greet(pipe=p_up)
    greet(pipe=p_down)

    drain(tokc, load_sem.at[0])

    def squares(ref, k, before):
        for j in range(nd):
            wide = ref[k, j].astype(F32)
            before = before + wide * wide
        return before

    def scale(t, squared):
        inverse[t] = lax.rsqrt(jnp.sum(squared, axis=-1, keepdims=True) / width + epsilon)

    def normalize(t, ref, k):
        for j in range(nd):
            norm[k, j] = (ref[k, j].astype(F32) * inverse[t] * gain_of(k, j)).astype(BF16)

    none = jnp.zeros((rows, kc), F32)
    scale(0, lax.fori_loop(0, nk, lambda k, c: squares(tokc, k, c), none))
    pl.semaphore_wait(barrier, nd - 1 + ne - 1 + 2)

    def work_out_places():
        row_tile = lax.broadcasted_iota(jnp.int32, (rows, rows), 1) // TILE
        row_at = lax.broadcasted_iota(jnp.int32, (1, rows), 1)
        earlier = (row_tile.T < row_tile)
        for t in range(PASSES):
            expert_of = jnp.broadcast_to(dest[t, 0:1, :], (rows, rows))
            same = jnp.where(earlier & (expert_of.T == expert_of), 1.0, 0.0).astype(F32)
            rank = jnp.sum(same, axis=0, keepdims=True) / TILE
            inner = (q * TILE + row_at % TILE).astype(F32)
            mine = dest[t, 0:1, :]
            dest_own[t] = jnp.broadcast_to(rank * lane + mine * unit + inner, (8, rows))
        for d in range(1, nd):
            send(dest_own, dest_all.at[q], dest_s, dest_r, dp=lax.rem(q + d, nd))
        dest_all[q] = dest_own[...]

    def build_places():
        drain(dest_all.at[0 : nd - 1], dest_r)
        slot_ids = lax.broadcasted_iota(jnp.int32, (total, rows), 0).astype(F32)
        for t in range(PASSES):
            for s in range(nd):
                hot = jnp.where(slot_ids == dest_all[s, t, 0:1, :], 1.0, 0.0).astype(F32)
                place[t, :, s * rows : (s + 1) * rows] = hot.astype(BF16)
                back[t, s * rows : (s + 1) * rows, :] = hot.T.astype(BF16)


    def y_send(ph, st, src, k):
        for d in range(1, nd):
            j = lax.rem(q + d, nd)
            send(src.at[k, j], yin.at[st, k, at(q, rows)], y_s.at[ph, k], y_r.at[ph, k], dp=j)
        yin[st, k, at(q, rows), :] = src[k, q]

    def y_wait(ph, st, k):
        drain(yin.at[st, k, 0 : (nd - 1) * rows], y_r.at[ph, k])

    def x_send(ph, st, t, k, g):
        mine = span_of(g)
        xout[k, mine, :] = jnp.dot(place[t, mine, :], yin[st, k], preferred_element_type=F32).astype(BF16)
        for d in range(1, ne):
            o = lax.rem(e + d, ne)
            send(xout.at[k, rows_of(g, o)], xin.at[ph, k, rows_of(g, e)], x_s.at[ph, k, g], x_r.at[ph, k, g], expert=o)
        xin[ph, k, rows_of(g, e), :] = xout[k, rows_of(g, e), :]

    def x_wait(ph, k, g):
        drain(xin.at[ph, k, 0 : (ne - 1) * unit], x_r.at[ph, k, g])

    def forward_chunk(ph, k, g):
        x_wait(ph, k, g)
        mine = span_of(g)
        acc[mine, :] += jnp.dot(xin[ph, k, mine, :], wgu[at(k, kc), :], preferred_element_type=F32)

    def backward_chunk(ph, k):
        for g in lanes:
            x_wait(ph, k, g)

        def some(m):
            there = at(m, lane)
            acc[there, 0:hidden] += lax.dot_general(
                xin[ph, k, there, :], wdc[k], (((1,), (1,)), ((), ())), preferred_element_type=F32
            )

        loop(CAP, some)

    def settle_y(ph, st):
        loop(nk, lambda k: drain(yin.at[st, k, 0 : (nd - 1) * rows], y_s.at[ph, k]))

    def settle_x(ph):
        def step(k):
            for g in lanes:
                drain(xout.at[k, 0 : (ne - 1) * unit], x_s.at[ph, k, g])

        loop(nk, step)

    def span(g, b, h):
        return pl.ds(pl.multiple_of(g * lane + (2 * b + h) * half, half), half)

    def summing(ph, src, one, two):
        def open_(g):
            send(src.at[span(g, q_far, 0)], one.at[g, 0], sum_s.at[ph, g, 0], one_r.at[ph, g, 0], dp=q_down)
            send(src.at[span(g, q_far, 1)], one.at[g, 1], sum_s.at[ph, g, 1], one_r.at[ph, g, 1], dp=q_up)
            send(src.at[span(g, q_down, 1)], two.at[g, 0, 1], sum_s.at[ph, g, 2], two_r.at[ph, g, 0, 1], dp=q_down)
            send(src.at[span(g, q_up, 0)], two.at[g, 1, 0], sum_s.at[ph, g, 3], two_r.at[ph, g, 1, 0], dp=q_up)

        def middle(g):
            for side, b in ((0, q_down), (1, q_up)):
                drain(one.at[g, side], one_r.at[ph, g, side])
                there = span(g, b, side)
                src[there, :] = (src[there, :].astype(F32) + one[g, side].astype(F32)).astype(BF16)
                send(src.at[there], two.at[g, side, side], sum_s.at[ph, g, 4 + side], two_r.at[ph, g, side, side], dp=b)

        def whole(g, h):
            for side in range(2):
                drain(two.at[g, side, h], two_r.at[ph, g, side, h])
            return src[span(g, q, h), :].astype(F32) + two[g, 0, h].astype(F32) + two[g, 1, h].astype(F32)

        def settle(g):
            for i in range(6):
                drain(src.at[0:half], sum_s.at[ph, g, i])

        return open_, middle, whole, settle

    def giving(ph, dst):
        def offer(g):
            for i in range(2):
                up, down = span(g, q, i), span(g, q, 1 - i)
                send(dst.at[up], dst.at[up], give_s.at[ph, g, i], give_r.at[ph, g, 0, i], dp=q_up)
                send(dst.at[down], dst.at[down], give_s.at[ph, g, 2 + i], give_r.at[ph, g, 1, 1 - i], dp=q_down)

        def pass_on(g):
            first, second = span(g, q_down, 0), span(g, q_up, 1)
            drain(dst.at[first], give_r.at[ph, g, 0, 0])
            send(dst.at[first], dst.at[first], give_s.at[ph, g, 4], give_r.at[ph, g, 2, 0], dp=q_up)
            drain(dst.at[second], give_r.at[ph, g, 1, 1])
            send(dst.at[second], dst.at[second], give_s.at[ph, g, 5], give_r.at[ph, g, 2, 1], dp=q_down)

        def close(g):
            drain(dst.at[span(g, q_down, 1)], give_r.at[ph, g, 0, 1])
            drain(dst.at[span(g, q_up, 0)], give_r.at[ph, g, 1, 0])
            drain(dst.at[span(g, q_far, 0)], give_r.at[ph, g, 2, 0])
            drain(dst.at[span(g, q_far, 1)], give_r.at[ph, g, 2, 1])

        def settle(g):
            for i in range(6):
                drain(dst.at[0:half], give_s.at[ph, g, i])

        return offer, pass_on, close, settle

    def small_steps(g, step):
        size = math.gcd(64, lane)
        lax.fori_loop(g * (lane // size), (g + 1) * (lane // size), lambda m, c: (step(at(m, size)), c)[1], 0)

    def round_into(src, columns, g):
        def some(there):
            src[there, :] = acc[there, 0:columns].astype(BF16)

        small_steps(g, some)

    def ret_send(ph, st, g, k):
        for d in range(1, ne):
            o = lax.rem(e + d, ne)
            send(
                ret_out.at[k, rows_of(g, o)], ret_in.at[st, k, rows_of(g, e)],
                rx_s.at[ph, k, g], rx_r.at[ph, k, g], expert=o,
            )
        ret_in[st, k, rows_of(g, e), :] = ret_out[k, rows_of(g, e), :]

    def settle_ret(ph, g):
        loop(nk, lambda k: drain(ret_out.at[k, 0 : (ne - 1) * unit], rx_s.at[ph, k, g]))

    def settle_yret(ph):
        loop(nk, lambda k: drain(yret_out.at[k, 0 : (nd - 1) * rows], ry_s.at[ph, k]))

    short = nd * rows // 2

    def collect_late(ph, st, t, k):
        for g in lanes:
            drain(ret_in.at[st, k, 0 : (ne - 1) * unit], rx_r.at[ph, k, g])
        for j in range(nd):
            norm[k, j] = jnp.dot(
                back[t, j * rows : (j + 1) * rows, :], ret_in[st, k], preferred_element_type=F32
            ).astype(BF16)
        for d in range(1, nd):
            j = lax.rem(q + d, nd)
            send(norm.at[k, j], yret_in.at[st, k, q], ry_s.at[ph, k], ry_r.at[ph, k], dp=j)
        yret_in[st, k, q] = norm[k, q]

    def collect(ph, st, t, k):
        for g in lanes:
            drain(ret_in.at[st, k, 0 : (ne - 1) * unit], rx_r.at[ph, k, g])

        def some(m):
            yret_out[k, at(m, short), :] = jnp.dot(
                back[t, at(m, short), :], ret_in[st, k], preferred_element_type=F32
            ).astype(BF16)

        loop(2, some)
        for d in range(1, nd):
            j = lax.rem(q + d, nd)
            send(yret_out.at[k, at(j, rows)], yret_in.at[st, k, q], ry_s.at[ph, k], ry_r.at[ph, k], dp=j)
        yret_in[st, k, q] = yret_out[k, at(q, rows), :]

    def landed(ph, st, k):
        drain(yret_in.at[st, k, 0 : nd - 1], ry_r.at[ph, k])

    def activate(t, g):
        def some(there):
            gate = gate_up[t, there, 0:hidden].astype(F32)
            up = gate_up[t, there, hidden : 2 * hidden].astype(F32)
            act[there, :] = (gate * jax.nn.sigmoid(gate) * up).astype(BF16)

        small_steps(g, some)

    def forward_down(ph, g):
        mine = span_of(g)

        def down(k):
            ret_out[k, mine, :] = jnp.dot(act[mine, :], wdc[k], preferred_element_type=F32).astype(BF16)
            ret_send(ph, 0, g, k)

        loop(nk, down)

    def turn(t):
        wide = math.gcd(total, 128)
        for m in range(total // wide):
            act_t[t, :, m * wide : (m + 1) * wide] = act[m * wide : (m + 1) * wide, :].T

    def pre_grads(gate, up, grad):
        s = jax.nn.sigmoid(gate)
        silu = gate * s
        return grad * up * s * (1.0 + gate * (1.0 - s)), grad * silu, silu * up

    def before(t, g):
        def some(there):
            gate = gate_up[t, there, 0:hidden].astype(F32)
            up = gate_up[t, there, hidden : 2 * hidden].astype(F32)
            of_gate, of_up, _ = pre_grads(gate, up, grad_act[there, :].astype(F32))
            gate_up[t, there, 0:hidden] = of_gate.astype(BF16)
            gate_up[t, there, hidden : 2 * hidden] = of_up.astype(BF16)

        small_steps(g, some)

    def backward_up(ph, t, g):
        mine = span_of(g)

        def up_(k):
            ret_out[k, mine, :] = lax.dot_general(
                gate_up[t, mine, :], wgu[at(k, kc), :], (((1,), (1,)), ((), ())), preferred_element_type=F32
            ).astype(BF16)
            ret_send(ph, 1, g, k)

        loop(nk, up_)

    def to_rows(ref, k, out, sem):
        for j in range(nd):
            cols = pl.ds(pl.multiple_of(j * quarter + k * kc, kc), kc)
            pltpu.make_async_copy(ref.at[k, j], out.at[:, cols], sem).start()

    def add_rows(ph, ref, k):
        landed(ph, 0, k)
        for j in range(nd):
            yret_in[0, k, j] = (ref[k, j].astype(F32) + yret_in[0, k, j].astype(F32)).astype(BF16)

    def terms(t, ref, k, j):
        return yret_in[1, k, j].astype(F32), ref[k, j].astype(F32) * inverse[t]

    def gather_grads(ph, t, ref, k):
        landed(ph, 1, k)
        fresh = mean_acc[...]
        for j in range(nd):
            u, scaled = terms(t, ref, k, j)
            both = u * scaled
            gain_acc[j, k] += jnp.sum(both.reshape(rows // 8, 8, kc), axis=0)
            fresh = fresh + both * gain_of(k, j)
        mean_acc[...] = fresh

    def finish_grads(t, ref, grad_ref, k, mean):
        for j in range(nd):
            u, scaled = terms(t, ref, k, j)
            wide = inverse[t] * (u * gain_of(k, j) - scaled * mean)
            yret_in[1, k, j] = (grad_ref[k, j].astype(F32) + wide).astype(BF16)

    def mean_of():
        return jnp.sum(mean_acc[...], axis=-1, keepdims=True) / width

    def weight_grads(k):
        both = jnp.zeros((kc, 2 * hidden), F32)
        for t in range(PASSES):
            both = both + lax.dot_general(
                xin[t, k], gate_up[t], (((0,), (0,)), ((), ())), preferred_element_type=F32
            )
        wgu[at(k, kc), :] = both.astype(BF16)
        pltpu.make_async_copy(wgu.at[at(k, kc), 0:hidden], gg.at[at(k, kc)], store_sem.at[2]).start()
        pltpu.make_async_copy(wgu.at[at(k, kc), hidden : 2 * hidden], gu.at[at(k, kc)], store_sem.at[2]).start()
        down = jnp.zeros((hidden, kc), F32)
        for t, ph in ((0, 3), (1, 2)):
            down = down + jnp.dot(act_t[t], xin[ph, k], preferred_element_type=F32)
        wdc[k] = down.astype(BF16)
        pltpu.make_async_copy(wdc.at[k], gd.at[:, at(k, kc)], store_sem.at[3]).start()

    def long_way(d, src, dst, where):
        def leave_():
            send(src, way.at[d, 0], z_s.at[d, 0], way_r.at[d, 0], pipe=where)

        def hop1():
            drain(way.at[d, 0], way_r.at[d, 0])
            send(way.at[d, 0], way.at[d, 1], way_s.at[d, 0], way_r.at[d, 1], pipe=where)

        def hop2():
            drain(way.at[d, 1], way_r.at[d, 1])
            send(way.at[d, 1], dst, way_s.at[d, 1], z_r.at[d, 0], pipe=where)

        return leave_, hop1, hop2

    def when(test, step):
        @pl.when(test)
        def _():
            step()

    lag = 2

    def forward_to_sums(ph, st, t, sums, mine, gives):
        open_, middle = sums[0], sums[1]
        acc[...] = jnp.zeros_like(acc)

        def step(i):
            for g in lanes:
                def first(g=g):
                    if g == 0:
                        y_wait(ph, st, i)
                    x_send(ph, st, t, i - g * lag, g)

                when((i >= g * lag) & (i < nk + g * lag), first)
            for g in lanes:
                when((i >= g * lag + 1) & (i < nk + g * lag + 1), lambda g=g: forward_chunk(ph, i - g * lag - 1, g))

        def start(g):
            round_into(rs_f, 2 * hidden, g)
            open_(g)

        def run(first, last):
            lax.fori_loop(first, last, lambda i, c: (step(i), c)[1], 0)

        run(0, nk + 1)
        start(0)
        run(nk + 1, nk + 2)
        middle(0)
        run(nk + 2, nk + 3)
        start(1)
        mine(0)
        run(nk + 3, nk + 4)
        gives[1](0)
        middle(1)
        run(nk + 4, nk + 5)
        start(2)
        mine(1)
        middle(2)

    def norm_out0(k):
        normalize(0, tokc, k)
        y_send(0, 0, norm, k)

    work_out_places()
    loop(nk, norm_out0)
    gain_acc[...] = jnp.zeros_like(gain_acc)
    build_places()
    drain(wgu, load_sem.at[1])
    drain(wdc, load_sem.at[2])
    drain(cotc, load_sem.at[3])

    sums = summing(0, rs_f, one_f, two_f)
    gives = giving(0, gate_up.at[0])

    def mine0(g):
        for h in range(2):
            gate_up[0, span(g, q, h), :] = sums[2](g, h).astype(BF16)
        gives[0](g)

    forward_to_sums(0, 0, 0, sums, mine0, gives)
    gives[2](0)
    activate(0, 0)
    forward_down(0, 0)
    gives[1](1)
    mine0(2)
    settle_y(0, 0)
    settle_x(0)
    gives[2](1)
    activate(0, 1)
    forward_down(0, 1)
    gives[1](2)
    acc[:, 0:hidden] = jnp.zeros((total, hidden), F32)
    gives[2](2)
    activate(0, 2)
    forward_down(0, 2)

    round0 = long_way(0, yret_in.at[0, 0], hid1.at[0], p_down)

    def turn_round(i):
        def second():
            k = i - 1
            add_rows(0, tokc, k)
            when(k == 0, round0[0])
            when(
                k > 0,
                lambda: send(yret_in.at[0, k], hid1.at[k], z_s.at[0, k], z_r.at[0, k], pipe=p_up),
            )
            y_wait(2, 1, k)
            for g in lanes:
                x_send(2, 1, 1, k, g)

        def first():
            collect(0, 0, 0, i)
            y_send(2, 1, cotc, i)

        when(i < nk, first)
        when((i >= 1) & (i <= nk), second)
        when(i >= 2, lambda: backward_chunk(2, i - 2))
        when(i == hop_at[0], round0[1])
        when(i == hop_at[1], round0[2])

    hop_at = (min(3, nk), min(5, nk + 1))
    loop(nk + 2, turn_round)
    sums_b = summing(2, rs_b, one_b, two_b)
    for g in lanes:
        round_into(rs_b, hidden, g)
        sums_b[0](g)
    turn(0)
    for g in lanes:
        sums[3](g)
        gives[3](g)
        settle_ret(0, g)
    settle_yret(0)
    settle_y(2, 1)
    settle_x(2)

    def arrived(k, c):
        drain(hid1.at[k], z_r.at[0, k])
        return squares(hid1, k, c)

    so_far = lax.fori_loop(1, nk, arrived, none)
    for g in lanes:
        sums_b[1](g)
    scale(1, arrived(0, so_far))
    loop(nk, lambda k: drain(yret_in.at[0, k], z_s.at[0, k]))

    def norm_out1(k):
        normalize(1, hid1, k)
        y_send(1, 0, norm, k)

    loop(nk, norm_out1)
    sums = summing(1, rs_f, one_f, two_f)
    gives = giving(1, gate_up.at[1])

    def mine1(g):
        for h in range(2):
            there = span(g, q, h)
            both = sums[2](g, h)
            of_gate, of_up, activated = pre_grads(both[:, 0:hidden], both[:, hidden : 2 * hidden], sums_b[2](g, h))
            gate_up[1, there, 0:hidden] = of_gate.astype(BF16)
            gate_up[1, there, hidden : 2 * hidden] = of_up.astype(BF16)
            act[there, :] = activated.astype(BF16)
        gives[0](g)

    forward_to_sums(1, 0, 1, sums, mine1, gives)

    gives[2](0)
    backward_up(2, 1, 0)
    gives[1](1)
    mine1(2)
    settle_y(1, 0)
    settle_x(1)
    gives[2](1)
    backward_up(2, 1, 1)
    gives[1](2)
    mean_acc[...] = jnp.zeros_like(mean_acc)
    gives[2](2)
    backward_up(2, 1, 2)

    def back1(i):
        when(i < nk, lambda: collect(2, 1, 1, i))
        when(i >= 1, lambda: gather_grads(2, 1, hid1, i - 1))

    loop(nk + 1, back1)
    mean = mean_of()

    round1 = long_way(1, yret_in.at[1, 0], grad0.at[0], p_up)

    def leave(k):
        finish_grads(1, hid1, cotc, k, mean)
        when(k == 0, round1[0])
        when(
            k > 0,
            lambda: send(yret_in.at[1, k], grad0.at[k], z_s.at[1, k], z_r.at[1, k], pipe=p_down),
        )

    loop(nk, leave)

    acts = giving(4, act)
    for g in lanes:
        acts[0](g)
    for g in lanes:
        sums[3](g)
        gives[3](g)
        sums_b[3](g)
        settle_ret(2, g)
    settle_yret(2)
    acc[:, 0:hidden] = jnp.zeros((total, hidden), F32)

    def come(i):
        def first():
            k = lax.rem(i + 1, nk)
            drain(grad0.at[k], z_r.at[1, k])
            y_send(3, 1, grad0, k)

        def second():
            k = lax.rem(i, nk)
            y_wait(3, 1, k)
            for g in lanes:
                x_send(3, 1, 0, k, g)

        when(i < nk, first)
        when((i >= 1) & (i <= nk), second)
        when(i >= 2, lambda: backward_chunk(3, lax.rem(i - 1, nk)))
        when(i == 1, round1[2])

    loop(1, come)
    round1[1]()
    for g in lanes:
        acts[1](g)
    for g in lanes:
        acts[2](g)
    lax.fori_loop(1, nk + 2, lambda i, c: (come(i), c)[1], 0)
    loop(nk, lambda k: drain(yret_in.at[1, k], z_s.at[1, k]))
    sums_b = summing(3, rs_b, one_b, two_b)
    gives = giving(3, grad_act)

    def mine3(g):
        for h in range(2):
            grad_act[span(g, q, h), :] = sums_b[2](g, h).astype(BF16)
        gives[0](g)

    for g in lanes:
        round_into(rs_b, hidden, g)
        sums_b[0](g)
    forward_down(1, 0)
    forward_down(1, 1)
    for g in lanes:
        sums_b[1](g)
    forward_down(1, 2)
    for g in lanes:
        mine3(g)
        if g >= 1:
            gives[1](g - 1)
    gives[1](CAP - 1)
    settle_y(3, 1)
    settle_x(3)
    for g in lanes:
        gives[2](g)
        before(0, g)
        settle_ret(1, g)
        backward_up(3, 0, g)

    turn(1)

    early = min(2, nk)
    loop(early, lambda k: collect_late(1, 0, 1, k))
    mean_acc[...] = jnp.zeros_like(mean_acc)

    def back0(i):
        when(i < nk, lambda: collect(3, 1, 0, i))
        when(i >= 1, lambda: gather_grads(3, 0, tokc, i - 1))
        when(i < nk - 1, lambda: weight_grads(i))

    loop(nk + 1, back0)
    for d in range(1, nd):
        j = lax.rem(q + d, nd)
        send(gain_acc.at[j], gain_dp.at[q], gain_s.at[0], gain_r.at[0], dp=j)
    lax.fori_loop(early, nk, lambda k, c: (collect_late(1, 0, 1, k), c)[1], 0)
    mean = mean_of()

    def last(k):
        finish_grads(0, tokc, grad0, k, mean)
        to_rows(yret_in.at[1], k, grad_tok, store_sem.at[1])

    loop(nk, last)

    gain_dp[q] = gain_acc[q]
    drain(gain_dp.at[0 : nd - 1], gain_r.at[0])
    mine = gain_dp[0]
    for j in range(1, nd):
        mine = mine + gain_dp[j]
    gain_ex[e] = mine
    for d in range(1, ne):
        send(gain_ex.at[e], gain_ex.at[e], gain_s.at[1], gain_r.at[1], expert=lax.rem(e + d, ne))
    weight_grads(nk - 1)

    def leave1(k):
        add_rows(1, hid1, k)
        to_rows(yret_in.at[0], k, out_tok, store_sem.at[0])

    loop(nk, leave1)
    drain(gain_ex.at[0 : ne - 1], gain_r.at[1])
    mine = gain_ex[0]
    for j in range(1, ne):
        mine = mine + gain_ex[j]
    gain_all[q] = mine
    for d in range(1, nd):
        send(gain_all.at[q], gain_all.at[q], gain_s.at[2], gain_r.at[2], dp=lax.rem(q + d, nd))
    drain(gain_all.at[0 : nd - 1], gain_r.at[2])
    gain_out[...] = jnp.broadcast_to(jnp.sum(gain_all[...], axis=2, keepdims=True), gain_out.shape)

    for g in lanes:
        sums_b[3](g)
        gives[3](g)
        acts[3](g)
        settle_ret(3, g)
    settle_yret(3)
    loop(nk, lambda k: drain(norm.at[k, 0 : nd - 1], ry_s.at[1, k]))
    for d in range(2):
        for i in range(2):
            drain(way.at[d, i], way_s.at[d, i])
    drain(gain_dp.at[0 : nd - 1], gain_s.at[0])
    drain(gain_ex.at[0 : ne - 1], gain_s.at[1])
    drain(gain_all.at[0 : nd - 1], gain_s.at[2])
    drain(dest_all.at[0 : nd - 1], dest_s)
    drain(yret_in.at[0], store_sem.at[0])
    drain(yret_in.at[1], store_sem.at[1])
    drain(wgu, store_sem.at[2])
    drain(wdc, store_sem.at[3])


def hand_over(quarter, kc, *refs):
    got, given, stages, sems = refs[0:6], refs[6:12], refs[12:17], refs[17]
    order = (3, 4, 5, 0, 1)

    def piece(n, h, way):
        size = stages[n].shape[0] // 2
        part = pl.ds(h * size, size)
        ends = (got[order[n]].at[part], stages[n].at[part], given[order[n]].at[part])
        return pltpu.make_async_copy(ends[way], ends[way + 1], sems.at[way, n, h])

    each = [(n, h) for n in range(len(order)) for h in range(2)]
    for n, h in each:
        piece(n, h, 0).start()
    for j in range(got[2].shape[0]):
        for k in range(got[2].shape[1]):
            given[2][0:1, j * quarter + k * kc : j * quarter + (k + 1) * kc] = got[2][j, k, 0:1, :]
    for n, h in each:
        piece(n, h, 0).wait()
        piece(n, h, 1).start()
    for n, h in each:
        piece(n, h, 1).wait()


def body(tokens, cotangent, gain, w_gate, w_up, w_down, route):
    npipe, nd, ne = lax.axis_size("pipe"), lax.axis_size("dp"), lax.axis_size("expert")
    section = lax.axis_index("pipe")
    rows, width = tokens.shape[1:]
    quarter, hidden = w_gate.shape[2:]
    kc = min(WIDTH, quarter)
    nk = quarter // kc
    block = nd * CAP * TILE
    total = ne * block
    half = total // CAP // nd // 2
    table = route[0, :, :, 0]
    dest = []
    for t in range(PASSES):
        micro = (section - t + npipe) % npipe
        now = lax.dynamic_index_in_dim(table, micro, 0, keepdims=False)
        dest.append(now.astype(F32))
    dest = jnp.broadcast_to(jnp.stack(dest)[:, None, :, None], (PASSES, 8, rows // TILE, TILE))
    dest = dest.reshape(PASSES, 8, rows)

    hbm = pl.BlockSpec(memory_space=pl.ANY)
    vmem = pl.BlockSpec(memory_space=pltpu.VMEM)
    V = pltpu.VMEM
    S = pltpu.SemaphoreType.DMA
    chunks = (nk, nd, rows, kc)
    results = pl.pallas_call(
        functools.partial(kernel, (nd, npipe, ne, rows, width, hidden)),
        out_shape=(
            jax.ShapeDtypeStruct((rows, width), BF16),
            jax.ShapeDtypeStruct((rows, width), BF16),
            jax.ShapeDtypeStruct((nd, nk, 8, kc), F32),
            jax.ShapeDtypeStruct((quarter, hidden), BF16),
            jax.ShapeDtypeStruct((quarter, hidden), BF16),
            jax.ShapeDtypeStruct((hidden, quarter), BF16),
        ),
        in_specs=[vmem, hbm, hbm, vmem, hbm, hbm, hbm],
        out_specs=(hbm, hbm, vmem, hbm, hbm, hbm),
        scratch_shapes=[
            V(chunks, BF16),
            V(chunks, BF16),
            V(chunks, BF16),
            V(chunks, BF16),
            V(chunks, BF16),
            V((quarter, 2 * hidden), BF16),
            V((nk, hidden, kc), BF16),
            V((PASSES, 8, rows), F32),
            V((nd, PASSES, 8, rows), F32),
            V((PASSES, total, nd * rows), BF16),
            V((PASSES, nd * rows, total), BF16),
            V((2, nk, nd * rows, kc), BF16),
            V((nk, total, kc), BF16),
            V((4, nk, total, kc), BF16),
            V((total, 2 * hidden), F32),
            V((PASSES, total, 2 * hidden), BF16),
            V((total, hidden), BF16),
            V((PASSES, hidden, total), BF16),
            V((total, hidden), BF16),
            V((total, 2 * hidden), BF16),
            V((total, hidden), BF16),
            V((CAP, 2, half, 2 * hidden), BF16),
            V((CAP, 2, half, hidden), BF16),
            V((CAP, 2, 2, half, 2 * hidden), BF16),
            V((CAP, 2, 2, half, hidden), BF16),
            V((nk, total, kc), BF16),
            V((2, nk, total, kc), BF16),
            V((nk, nd * rows, kc), BF16),
            V((2,) + chunks, BF16),
            V((PASSES, rows, 1), F32),
            V((rows, kc), F32),
            V((nd, nk, 8, kc), F32),
            V((nd, nk, 8, kc), F32),
            V((ne, nk, 8, kc), F32),
            V((nd, nk, 8, kc), F32),
            V((2, 2) + chunks[1:], BF16),
            S((4,)),
            S((4,)),
            S(()),
            S(()),
            S((4, nk)),
            S((4, nk)),
            S((4, nk, CAP)),
            S((4, nk, CAP)),
            S((4, nk, CAP)),
            S((4, nk, CAP)),
            S((4, nk)),
            S((4, nk)),
            S((2, nk)),
            S((2, nk)),
            S((2, 2)),
            S((2, 2)),
            S((4, CAP, 6)),
            S((4, CAP, 2)),
            S((4, CAP, 2, 2)),
            S((5, CAP, 6)),
            S((5, CAP, 3, 2)),
            S((3,)),
            S((3,)),
        ],
        compiler_params=pltpu.CompilerParams(
            collective_id=0, has_side_effects=True, vmem_limit_bytes=63_000_000
        ),
        cost_estimate=pl.CostEstimate(
            flops=36 * total * quarter * hidden, bytes_accessed=17 * 2**20, transcendentals=2 * total * hidden
        ),
    )(dest, tokens[0], cotangent[0], gain, w_gate[0, 0], w_up[0, 0], w_down[0, 0])
    out_rows, entry_grad, gain_total, grad_gate, grad_up, grad_down = pl.pallas_call(
        functools.partial(hand_over, quarter, kc),
        out_shape=(
            results[0],
            results[1],
            jax.ShapeDtypeStruct((1, width), F32),
            results[3],
            results[4],
            results[5],
        ),
        in_specs=[hbm, hbm, vmem, hbm, hbm, hbm],
        out_specs=(hbm, hbm, vmem, hbm, hbm, hbm),
        scratch_shapes=[V(results[i].shape, BF16) for i in (3, 4, 5, 0, 1)] + [S((2, 5, 2))],
        compiler_params=pltpu.CompilerParams(vmem_limit_bytes=40_000_000),
    )(*results)
    return (
        out_rows[None],
        entry_grad[None],
        gain_total,
        grad_gate[None, None],
        grad_up[None, None],
        grad_down[None, None],
    )


def solution(mesh):
    placed = (
        P("pipe", ("dp", "expert"), None),
        P("pipe", ("dp", "expert"), None),
        P("pipe", None),
        P("pipe", "expert", "dp", None),
        P("pipe", "expert", "dp", None),
        P("pipe", "expert", None, "dp"),
        P("pipe", None, ("dp", "expert"), None),
    )
    return jax.shard_map(
        body,
        mesh=mesh,
        in_specs=placed,
        out_specs=(
            P("pipe", ("dp", "expert"), None),
            P("pipe", ("dp", "expert"), None),
            P("pipe", None),
            P("pipe", "expert", "dp", None),
            P("pipe", "expert", "dp", None),
            P("pipe", "expert", None, "dp"),
        ),
        check_vma=False,
    )
```
